32 devices in a mesh: group: 8 (over y, x, core), tensor: 4 (over z).
Axes of the slice: x: 2, y: 2, z: 4, core: 2. Of those that a mesh axis runs over, the one named last changes fastest.
Arguments:
- queries: bfloat16 [3072, 4096], P('group', 'tensor')
- text_kv: bfloat16 [3072, 2048], P('group', 'tensor')
- out_grad: bfloat16 [3072, 4096], P('group', 'tensor'), may hold values from -6 to 6
- text_segment: int32 [8, 384], P('group'), may hold values from 0 to 7, never falling along the last dimension, each value on 1 to 96 neighbouring positions
- visual_rows: bfloat16 [1024, 8192], P('group', 'tensor'), may hold values from -6 to 6
- kv_weight: bfloat16 [8192, 2048], P('tensor'), may hold values from -0.0625 to 0.0625
- visual_dest: int32 [1024, 1], P('group'), may hold values from 0 to 7, as said below
- visual_sample: int32 [1024], P('group'), may hold values from 0 to 7, as said below
Outputs:
- attended: bfloat16 [3072, 4096], P('group', 'tensor')
- query_grad: bfloat16 [3072, 4096], P('group', 'tensor')
- text_kv_grad: bfloat16 [3072, 2048], P('group', 'tensor')
- visual_grad: bfloat16 [1024, 8192], P('group', 'tensor')
The draws below stay inside these ranges and needn't reach their ends.
Inputs may be any that keep to these rules, and one draw needn't show every extreme that they name: `visual_dest`: a group's rows come in aligned runs of 32 rows, each run to one pack, the runs of one group to distinct packs, so exactly 32 rows of a group reach each pack that it names and none reach the others. `visual_sample`: one sample for all rows of a run. `text_segment`: never falling along a pack, each sample at most 96 tokens.
All inputs are finite; a program needn't handle non-finite values.
Results may differ from the reference program's by a relative error of at most 0.015.
Values may be sent and summed in bfloat16 or wider, within the bound.
No kernel may reach another device: no remote copies, remote signals or barrier semaphores. Data moves between devices by JAX's collectives and lax.ppermute only.
A program may use at most 64 MiB of HBM per device.

```python
import math
import jax
import jax.numpy as jnp
import numpy as np
from jax import lax

D = 8192
KVH = 8
HD = 128
QPK = 4
QH = 32
PACK = 384
VIS_DEV = 128
SEGS = 8
SEG_MOST = 96
CAP = 32
TEXT = 3072
VIS = 1024
N_GROUP = 8


def text_pair(key):
    base = jax.random.fold_in(key, 11)
    kv_full = jax.random.normal(jax.random.fold_in(base, 1), (TEXT, 2 * KVH * HD), jnp.float32)
    query_full = jax.random.normal(jax.random.fold_in(base, 2), (TEXT, QPK * KVH * HD), jnp.float32)
    return (query_full, kv_full)


def draw_queries(key, part):
    return text_pair(key)[0].astype(jnp.bfloat16)


def draw_text_kv(key, part):
    return text_pair(key)[1].astype(jnp.bfloat16)


def draw_visual_dest(key, part):
    base = jax.random.fold_in(key, 23)
    run_count = VIS_DEV // CAP
    group_keys = jax.random.split(jax.random.fold_in(base, 1), N_GROUP)
    orders = jax.vmap(lambda one: jax.random.permutation(one, N_GROUP))(group_keys)[:, :run_count]
    return jnp.repeat(orders.astype(jnp.int32), CAP, axis=1).reshape(VIS, 1)


def draw_visual_sample(key, part):
    base = jax.random.fold_in(key, 29)
    run_count = VIS_DEV // CAP
    samples = jax.random.randint(jax.random.fold_in(base, 1), (N_GROUP * run_count,), 0, SEGS, dtype=jnp.int32)
    return jnp.repeat(samples, CAP).astype(jnp.int32)


def level_of(rng, extent, cuts, low, largest):
    def one(axis_at, shards_of):
        draws = jax.random.uniform(jax.random.fold_in(jax.random.fold_in(rng, 6), axis_at), (shards_of,), jnp.float32, low / len(cuts), largest / len(cuts))
        return jnp.repeat(jnp.exp(draws), extent[axis_at] // shards_of).reshape((-1,) + (1,) * (len(extent) - axis_at - 1))

    gain = one(*cuts[0])
    for cut in cuts[1:]:
        gain = gain * one(*cut)
    return gain


def split_up(number_of, total, reach, skew):
    portions = [(1 << 20) // math.isqrt(grade ** skew) + 1 for grade in range(2, number_of + 1)]
    surplus, given = total - reach - (number_of - 1), [1] * (number_of - 1)
    while surplus > 0:
        free = [i for i in range(number_of - 1) if given[i] < reach]
        pool, budget = sum([portions[i] for i in free]), surplus
        for i in free:
            more = min(reach - given[i], max(1, budget * portions[i] // pool), surplus)
            given[i] = given[i] + more
            surplus = surplus - more
    return np.array([reach] + given)


def uneven(rng, number_of, total, limit, slope):
    if number_of == 2:
        one = jax.random.randint(rng, (), max(1, total - limit), min(limit, total - 1) + 1)
        return jnp.stack([one, total - one])
    tallies = jnp.asarray(split_up(number_of, total, limit, slope), jnp.int32)
    pairs = (number_of - 1) // 2
    donor, taker = tallies[1:1 + 2 * pairs:2], tallies[2:2 + 2 * pairs:2]
    room = jnp.minimum(donor - 1, limit - taker)
    moved = jax.random.randint(jax.random.fold_in(rng, 1), (pairs,), 0, 1 << 20) % (room + 1)
    tallies = tallies.at[1:1 + 2 * pairs:2].set(donor - moved).at[2:2 + 2 * pairs:2].set(taker + moved)
    return tallies[jax.random.permutation(jax.random.fold_in(rng, 2), number_of)]


def bell_draw(rng, dims, deviation, bound, cuts=(), kind=jnp.bfloat16):
    factor_of = level_of(rng, dims, cuts, -0.22, 0.18) if cuts else 1.0
    entries = jax.random.normal(rng, dims, jnp.float32) * deviation * factor_of
    return jnp.minimum(jnp.maximum(entries, -bound), bound).astype(kind)


def setup_inputs(seed: int = 0) -> dict:
    arg_keys = jax.random.split(jax.random.key(seed), 9)
    queries = draw_queries(jax.random.fold_in(arg_keys[8], 71), 0)
    text_kv = draw_text_kv(jax.random.fold_in(arg_keys[8], 71), 0)
    out_grad = bell_draw(arg_keys[2], (TEXT, QH * HD), 1.0, 6.0, ((0, 8), (1, 4)))
    text_segment = jax.vmap(lambda own: jnp.searchsorted(jnp.cumsum(uneven(own, SEGS, PACK, SEG_MOST, 1)), jnp.arange(PACK), side="right"))(jax.random.split(arg_keys[3], N_GROUP)).reshape((N_GROUP, PACK)).astype(jnp.int32)
    visual_rows = bell_draw(arg_keys[4], (VIS, D), 1.0, 6.0, ((0, 8), (1, 4)))
    kv_weight = bell_draw(arg_keys[5], (D, 2 * KVH * HD), D ** -0.5, 0.0625, ((0, 4),))
    visual_dest = draw_visual_dest(jax.random.fold_in(arg_keys[8], 71), 0)
    visual_sample = draw_visual_sample(jax.random.fold_in(arg_keys[8], 71), 0)
    return {"queries": queries, "text_kv": text_kv, "out_grad": out_grad, "text_segment": text_segment, "visual_rows": visual_rows, "kv_weight": kv_weight, "visual_dest": visual_dest, "visual_sample": visual_sample}


def to_bf16_and_back(values):
    return lax.optimization_barrier(values.astype(jnp.bfloat16)).astype(jnp.float32)

def slot_index(visual_dest):
    destination = visual_dest[:, 0].reshape(N_GROUP, VIS_DEV)
    onehot = (destination[:, :, None] == jnp.arange(N_GROUP, dtype=jnp.int32)[None, None, :]).astype(jnp.int32)
    earlier = jnp.cumsum(onehot, axis=1) - onehot
    rank = lax.optimization_barrier(jnp.sum(earlier * onehot, axis=2))
    source = jnp.arange(N_GROUP, dtype=jnp.int32)[:, None]
    slot = source * CAP + rank
    return (destination.reshape(-1).astype(jnp.int32), slot.reshape(-1).astype(jnp.int32))

def attend_pack(pack):
    queries, text_kv, out_grad, segment, vis_kv, vis_sample = pack
    length = queries.shape[0]
    scale = 1.0 / math.sqrt(HD)
    query_heads = queries.astype(jnp.float32).reshape(length, KVH, QPK, HD)
    grad_heads = out_grad.astype(jnp.float32).reshape(length, KVH, QPK, HD)
    text_heads = text_kv.reshape(length, KVH, 2, HD)
    vis_heads = vis_kv.reshape(vis_kv.shape[0], KVH, 2, HD)
    keys = jnp.concatenate([text_heads[:, :, 0], vis_heads[:, :, 0]], axis=0).astype(jnp.float32)
    values = jnp.concatenate([text_heads[:, :, 1], vis_heads[:, :, 1]], axis=0).astype(jnp.float32)
    places = jnp.arange(length, dtype=jnp.int32)
    text_mask = (segment[:, None] == segment[None, :]) & (places[None, :] <= places[:, None])
    vis_mask = vis_sample[None, :] == segment[:, None]
    mask = jnp.concatenate([text_mask, vis_mask], axis=1)
    scores = jnp.einsum('pgjd,kgd->gjpk', query_heads, keys) * scale
    top = lax.optimization_barrier(jnp.max(jnp.where(mask, scores, -jnp.inf), axis=-1, keepdims=True))
    expo = jnp.where(mask, jnp.exp(scores - top), 0.0)
    probs = expo / lax.optimization_barrier(jnp.sum(expo, axis=-1, keepdims=True))
    weights = to_bf16_and_back(probs)
    attended = jnp.einsum('gjpk,kgd->pgjd', weights, values).astype(jnp.bfloat16)
    dprobs = jnp.einsum('pgjd,kgd->gjpk', grad_heads, values)
    inner = lax.optimization_barrier(jnp.sum(probs * dprobs, axis=-1, keepdims=True))
    dscores = to_bf16_and_back(probs * (dprobs - inner) * scale)
    query_grad = jnp.einsum('gjpk,kgd->pgjd', dscores, keys).astype(jnp.bfloat16)
    key_grad = jnp.einsum('gjpk,pgjd->kgd', dscores, query_heads).astype(jnp.bfloat16)
    value_grad = jnp.einsum('gjpk,pgjd->kgd', weights, grad_heads).astype(jnp.bfloat16)
    kv_grad = jnp.stack([key_grad, value_grad], axis=2)
    text_grad = kv_grad[:length].reshape(length, -1)
    vis_grad = kv_grad[length:].reshape(vis_kv.shape[0], -1)
    return (attended.reshape(length, -1), query_grad.reshape(length, -1), text_grad, vis_grad)

def reference(queries, text_kv, out_grad, text_segment, visual_rows, kv_weight, visual_dest, visual_sample):
    visual_kv = jnp.dot(visual_rows, kv_weight, preferred_element_type=jnp.float32).astype(jnp.bfloat16)
    destination, slot = slot_index(visual_dest)
    width = visual_kv.shape[1]
    buffer = jnp.zeros((N_GROUP, N_GROUP * CAP, width), jnp.bfloat16).at[destination, slot].set(visual_kv)
    tags = jnp.full((N_GROUP, N_GROUP * CAP), -1, jnp.int32).at[destination, slot].set(visual_sample)
    packs = (queries.reshape(N_GROUP, PACK, -1), text_kv.reshape(N_GROUP, PACK, -1), out_grad.reshape(N_GROUP, PACK, -1), text_segment, buffer, tags)
    attended, query_grad, text_grad, vis_grad = lax.map(attend_pack, packs)
    visual_kv_grad = vis_grad[destination, slot]
    visual_grad = jnp.dot(visual_kv_grad, kv_weight.T, preferred_element_type=jnp.float32).astype(jnp.bfloat16)
    return (attended.reshape(TEXT, -1), query_grad.reshape(TEXT, -1), text_grad.reshape(TEXT, -1), visual_grad)
```

```python
import functools
import math

import jax
import jax.numpy as jnp
from jax import lax
from jax.experimental import pallas as pl
from jax.experimental.pallas import tpu as pltpu
from jax.sharding import PartitionSpec as P

HD = 128
QPK = 4
TILE = 128
SCALE = 1.0 / math.sqrt(HD)
LOG2E = math.log2(math.e)
F32 = jnp.float32
BF16 = jnp.bfloat16
MIB = 1024 * 1024


def dot_nn(a, b):
    return lax.dot_general(a, b, (((1,), (0,)), ((), ())), preferred_element_type=F32)


def dot_nt(a, b):
    return lax.dot_general(a, b, (((1,), (1,)), ((), ())), preferred_element_type=F32)


def dot_tn(a, b):
    return lax.dot_general(a, b, (((0,), (0,)), ((), ())), preferred_element_type=F32)


def params(mib):
    return pltpu.CompilerParams(vmem_limit_bytes=mib * MIB)


def cost(flops, moved, exps=0):
    return pl.CostEstimate(flops=flops, bytes_accessed=moved, transcendentals=exps)


def project_kernel(order_ref, rows_ref, weight_ref, *refs, steps):
    outs, total = refs[:-1], refs[-1]
    block, step = pl.program_id(0), pl.program_id(1)
    depth = weight_ref.shape[0]
    part = dot_nn(rows_ref[:, pl.ds(pl.multiple_of(step * depth, depth), depth)], weight_ref[...])

    @pl.when(step == 0)
    def _():
        total[...] = part

    @pl.when(step > 0)
    def _():
        total[...] += part

    for at, out in enumerate(outs):

        @pl.when((step == steps - 1) & (block == at))
        def _(out=out):
            out[...] = total[...].astype(out.dtype)


def project(order, rows, weight, width, kinds):
    count, features = rows.shape
    steps = 4
    depth = features // steps
    whole = pl.BlockSpec((count, width), lambda i, k, order: (0, 0))
    return pl.pallas_call(
        functools.partial(project_kernel, steps=steps),
        out_shape=[jax.ShapeDtypeStruct((count, width), kind) for kind in kinds],
        grid_spec=pltpu.PrefetchScalarGridSpec(
            num_scalar_prefetch=1,
            grid=(len(kinds), steps),
            in_specs=[
                pl.BlockSpec((count, features), lambda i, k, order: (0, 0)),
                pl.BlockSpec((depth, width), lambda i, k, order: (k, order[i])),
            ],
            out_specs=[whole for _ in kinds],
            scratch_shapes=[pltpu.VMEM((count, width), F32)],
        ),
        compiler_params=params(12),
        cost_estimate=cost(
            2 * count * features * width * len(kinds), 2 * features * width * len(kinds)
        ),
        name="project",
    )(order, rows, weight)


def place_kernel(me_ref, dest_ref, sample_ref, own_ref, *refs, capacity, flips):
    parts, outs = refs[: -len(flips)], refs[-len(flips) :]
    total = own_ref[...]
    for part in parts:
        total = total + part[...].astype(F32)
    tags = jnp.broadcast_to(sample_ref[...] + 1, (total.shape[0], TILE)).astype(F32)
    wide = jnp.concatenate([total, tags], axis=1).astype(BF16)
    rows = total.shape[0]
    for out, targets in zip(outs, flips, strict=True):
        slots = len(targets) * capacity
        slot = lax.broadcasted_iota(jnp.int32, (slots, rows), 0)
        row = lax.broadcasted_iota(jnp.int32, (slots, rows), 1)
        target = jnp.zeros((slots, rows), jnp.int32)
        if len(targets) > 8:
            target = slot // capacity
        else:
            for at, flip in enumerate(targets):
                target = jnp.where(slot // capacity == at, me_ref[0] ^ flip, target)
        select = (dest_ref[...] == target) & (slot % capacity == row % capacity)
        out[...] = dot_nn(select.astype(F32).astype(BF16), wide).astype(BF16)


def place(me, dest_row, sample_col, own, parts, capacity, flips):
    rows, width = own.shape
    vmem = pl.BlockSpec(memory_space=pltpu.VMEM)
    return pl.pallas_call(
        functools.partial(place_kernel, capacity=capacity, flips=flips),
        out_shape=[
            jax.ShapeDtypeStruct((len(f) * capacity, width + TILE), BF16) for f in flips
        ],
        in_specs=[pl.BlockSpec(memory_space=pltpu.SMEM)] + [vmem] * (3 + len(parts)),
        out_specs=[vmem] * len(flips),
        compiler_params=params(8),
        cost_estimate=cost(2 * 256 * rows * width, 4 * rows * width),
        name="place",
    )(me, dest_row, sample_col, own, *parts)


def collect_kernel(me_ref, dest_ref, *refs, capacity, flips):
    parts, out = refs[:-1], refs[-1]
    rows = out.shape[0]
    total = jnp.zeros(out.shape, F32)
    for part, targets in zip(parts, flips, strict=True):
        slots = len(targets) * capacity
        slot = lax.broadcasted_iota(jnp.int32, (rows, slots), 1)
        row = lax.broadcasted_iota(jnp.int32, (rows, slots), 0)
        target = jnp.zeros((rows, slots), jnp.int32)
        if len(targets) > 8:
            target = slot // capacity
        else:
            for at, flip in enumerate(targets):
                target = jnp.where(slot // capacity == at, me_ref[0] ^ flip, target)
        select = (dest_ref[...] == target) & (slot % capacity == row % capacity)
        total = total + dot_nn(select.astype(F32).astype(BF16), part[...])
    out[...] = total.astype(BF16)


def collect(me, dest_col, parts, capacity, flips):
    rows, width = dest_col.shape[0], parts[0].shape[1]
    vmem = pl.BlockSpec(memory_space=pltpu.VMEM)
    return pl.pallas_call(
        functools.partial(collect_kernel, capacity=capacity, flips=flips),
        out_shape=jax.ShapeDtypeStruct((rows, width), BF16),
        in_specs=[pl.BlockSpec(memory_space=pltpu.SMEM)] + [vmem] * (1 + len(parts)),
        out_specs=vmem,
        compiler_params=params(8),
        cost_estimate=cost(2 * 256 * rows * width, 4 * rows * width),
        name="collect",
    )(me, dest_col, *parts)


def stacked(ref, tile, head):
    first = head * QPK * HD
    return jnp.concatenate(
        [
            ref[tile * TILE : (tile + 1) * TILE, first + j * HD : first + (j + 1) * HD]
            for j in range(QPK)
        ],
        axis=0,
    )


def text_span(tile):
    return max(0, tile - 1) * TILE, (tile + 1) * TILE


def text_mask(segment_ref, tile):
    low, high = text_span(tile)
    span = high - low
    own = segment_ref[:, tile * TILE : (tile + 1) * TILE].astype(F32)
    keys = jnp.concatenate(
        [
            jnp.broadcast_to(segment_ref[:, at : at + TILE].astype(F32), (TILE, TILE)).T
            for at in range(low, high, TILE)
        ],
        axis=0,
    )
    key_place = lax.broadcasted_iota(jnp.int32, (span, TILE), 0) + low
    token_place = lax.broadcasted_iota(jnp.int32, (span, TILE), 1) + tile * TILE
    mask = (keys == own) & (key_place <= token_place)
    return jnp.where(mask, 0.0, -jnp.inf)


def slot_mask(tags, segment_ref, tile):
    own = segment_ref[:, tile * TILE : (tile + 1) * TILE].astype(F32) + 1.0
    return jnp.where(tags.astype(F32) == own, 0.0, -jnp.inf)


def repeated(mask):
    return jnp.concatenate([mask] * QPK, axis=1)


def text_stats_kernel(query_ref, grad_ref, kv_ref, segment_ref, top_ref, sum_ref, inner_ref):
    tiles, heads = query_ref.shape[0] // TILE, kv_ref.shape[1] // (2 * HD)
    for tile in range(tiles):
        low, high = text_span(tile)
        mask = repeated(text_mask(segment_ref, tile))
        for head in range(heads):
            at = head * tiles + tile
            keys = kv_ref[low:high, head * 2 * HD : head * 2 * HD + HD]
            values = kv_ref[low:high, head * 2 * HD + HD : (head + 1) * 2 * HD]
            scores = dot_nt(keys, stacked(query_ref, tile, head)) + mask
            top = jnp.max(scores, axis=0, keepdims=True)
            expo = jnp.exp2((scores - top) * (SCALE * LOG2E))
            dprobs = dot_nt(values, stacked(grad_ref, tile, head))
            top_ref[at : at + 1, :] = top
            sum_ref[at : at + 1, :] = jnp.sum(expo, axis=0, keepdims=True)
            inner_ref[at : at + 1, :] = jnp.sum(expo * dprobs, axis=0, keepdims=True)


def text_stats(queries, out_grad, text_kv, segment):
    tiles, heads = queries.shape[0] // TILE, text_kv.shape[1] // (2 * HD)
    vmem = pl.BlockSpec(memory_space=pltpu.VMEM)
    shape = jax.ShapeDtypeStruct((tiles * heads, QPK * TILE), F32)
    pairs = heads * QPK * (2 * tiles - 1) * TILE * TILE
    return pl.pallas_call(
        text_stats_kernel,
        out_shape=[shape] * 3,
        in_specs=[vmem] * 4,
        out_specs=[vmem] * 3,
        compiler_params=params(24),
        cost_estimate=cost(4 * pairs * HD, 4 * queries.size, pairs),
        name="text_stats",
    )(queries, out_grad, text_kv, segment)


def slot_grad_kernel(
    query_ref, grad_ref, segment_ref, top_ref, sum_ref, inner_ref, *refs, arrivals
):
    visual, refs = refs[:arrivals], refs[arrivals:]
    outs, (all_top_ref, scale_ref, all_inner_ref) = refs[:arrivals], refs[arrivals:]
    tiles = query_ref.shape[0] // TILE
    width = visual[0].shape[1] - TILE
    heads = width // (2 * HD)
    tags = jnp.concatenate([one[:, width:] for one in visual], axis=0)
    masks = [slot_mask(tags, segment_ref, tile) for tile in range(tiles)]
    for head in range(heads):
        first = head * 2 * HD
        keys = jnp.concatenate([one[:, first : first + HD] for one in visual], axis=0)
        values = jnp.concatenate([one[:, first + HD : first + 2 * HD] for one in visual], axis=0)
        key_grad = jnp.zeros((keys.shape[0], HD), F32)
        value_grad = jnp.zeros((keys.shape[0], HD), F32)
        for tile in range(tiles):
            at = head * tiles + tile
            query, grad = stacked(query_ref, tile, head), stacked(grad_ref, tile, head)
            scores = dot_nt(keys, query) + repeated(masks[tile])
            dprobs = dot_nt(values, grad)
            text_top = top_ref[at : at + 1, :]
            top = jnp.maximum(text_top, jnp.max(scores, axis=0, keepdims=True))
            expo = jnp.exp2((scores - top) * (SCALE * LOG2E))
            shift = jnp.exp2((text_top - top) * (SCALE * LOG2E))
            total = sum_ref[at : at + 1, :] * shift + jnp.sum(expo, axis=0, keepdims=True)
            inverse = 1.0 / total
            inner = (
                inner_ref[at : at + 1, :] * shift + jnp.sum(expo * dprobs, axis=0, keepdims=True)
            ) * inverse
            probs = expo * inverse
            dscores = (probs * (dprobs - inner)).astype(BF16)
            value_grad = value_grad + dot_nn(probs.astype(BF16), grad)
            key_grad = key_grad + dot_nn(dscores, query)
            all_top_ref[at : at + 1, :] = top
            scale_ref[at : at + 1, :] = inverse
            all_inner_ref[at : at + 1, :] = inner
        start = 0
        for out in outs:
            count = out.shape[0]
            out[:, first : first + HD] = (key_grad[start : start + count] * SCALE).astype(BF16)
            out[:, first + HD : first + 2 * HD] = value_grad[start : start + count].astype(BF16)
            start += count


def slot_grad(queries, out_grad, segment, stats, visual):
    vmem = pl.BlockSpec(memory_space=pltpu.VMEM)
    shape = jax.ShapeDtypeStruct(stats[0].shape, F32)
    slots = sum(one.shape[0] for one in visual)
    pairs = slots * queries.shape[0] * queries.shape[1] // HD
    found = pl.pallas_call(
        functools.partial(slot_grad_kernel, arrivals=len(visual)),
        out_shape=[
            jax.ShapeDtypeStruct((one.shape[0], one.shape[1] - TILE), BF16) for one in visual
        ]
        + [shape] * 3,
        in_specs=[vmem] * (6 + len(visual)),
        out_specs=[vmem] * (3 + len(visual)),
        compiler_params=params(24),
        cost_estimate=cost(8 * pairs * HD, 4 * queries.size, pairs),
        name="slot_grad",
    )(queries, out_grad, segment, *stats, *visual)
    return found[: len(visual)], found[len(visual) :]


def text_grad_kernel(
    query_ref, grad_ref, kv_ref, segment_ref, top_ref, scale_ref, inner_ref, *refs, arrivals
):
    visual = refs[:arrivals]
    attended_ref, query_grad_ref, kv_grad_ref = refs[arrivals:]
    tiles, heads = query_ref.shape[0] // TILE, kv_ref.shape[1] // (2 * HD)
    width = kv_ref.shape[1]
    tags = jnp.concatenate([one[:, width:] for one in visual], axis=0)
    masks = [
        jnp.concatenate(
            [text_mask(segment_ref, tile), slot_mask(tags, segment_ref, tile)], axis=0
        )
        for tile in range(tiles)
    ]
    for head in range(heads):
        first = head * 2 * HD
        slot_keys = jnp.concatenate([one[:, first : first + HD] for one in visual], axis=0)
        slot_values = jnp.concatenate(
            [one[:, first + HD : first + 2 * HD] for one in visual], axis=0
        )
        key_held = value_held = None
        for tile in range(tiles):
            at = head * tiles + tile
            low, high = text_span(tile)
            keys = jnp.concatenate([kv_ref[low:high, first : first + HD], slot_keys], axis=0)
            values = jnp.concatenate(
                [kv_ref[low:high, first + HD : first + 2 * HD], slot_values], axis=0
            )
            query, grad = stacked(query_ref, tile, head), stacked(grad_ref, tile, head)
            scores = dot_nt(keys, query) + repeated(masks[tile])
            expo = jnp.exp2((scores - top_ref[at : at + 1, :]) * (SCALE * LOG2E))
            probs = expo * scale_ref[at : at + 1, :]
            dprobs = dot_nt(values, grad)
            dscores = (probs * (dprobs - inner_ref[at : at + 1, :])).astype(BF16)
            weights = probs.astype(BF16)
            attended = dot_tn(values, weights)
            query_grad = dot_tn(keys, dscores) * SCALE
            place_at = slice(tile * TILE, (tile + 1) * TILE)
            for j in range(QPK):
                columns = slice((head * QPK + j) * HD, (head * QPK + j + 1) * HD)
                lanes = slice(j * TILE, (j + 1) * TILE)
                attended_ref[place_at, columns] = attended[:, lanes].T.astype(BF16)
                query_grad_ref[place_at, columns] = query_grad[:, lanes].T.astype(BF16)
            key_part = dot_nn(dscores[: high - low], query)
            value_part = dot_nn(weights[: high - low], grad)
            if tile > 0:
                before = slice((tile - 1) * TILE, tile * TILE)
                kv_grad_ref[before, first : first + HD] = (
                    (key_held + key_part[:TILE]) * SCALE
                ).astype(BF16)
                kv_grad_ref[before, first + HD : first + 2 * HD] = (
                    value_held + value_part[:TILE]
                ).astype(BF16)
            key_held, value_held = key_part[high - low - TILE :], value_part[high - low - TILE :]
        last = slice((tiles - 1) * TILE, tiles * TILE)
        kv_grad_ref[last, first : first + HD] = (key_held * SCALE).astype(BF16)
        kv_grad_ref[last, first + HD : first + 2 * HD] = value_held.astype(BF16)


def text_grad(queries, out_grad, text_kv, segment, stats, visual):
    vmem = pl.BlockSpec(memory_space=pltpu.VMEM)
    slots = sum(one.shape[0] for one in visual)
    pairs = (slots + 2 * TILE) * queries.shape[0] * queries.shape[1] // HD
    return pl.pallas_call(
        functools.partial(text_grad_kernel, arrivals=len(visual)),
        out_shape=[
            jax.ShapeDtypeStruct(queries.shape, BF16),
            jax.ShapeDtypeStruct(queries.shape, BF16),
            jax.ShapeDtypeStruct(text_kv.shape, BF16),
        ],
        in_specs=[vmem] * (7 + len(visual)),
        out_specs=[vmem] * 3,
        compiler_params=params(32),
        cost_estimate=cost(12 * pairs * HD, 8 * queries.size, pairs),
        name="text_grad",
    )(queries, out_grad, text_kv, segment, *stats, *visual)


def feature_kernel(order_ref, *refs, count, held, last):
    parts, (weight_ref, *rest) = refs[:count], refs[count:]
    before_ref = rest[0] if held else None
    out_ref, total = rest[-2], rest[-1]
    step = pl.program_id(0)
    for at, part in enumerate(parts):

        @pl.when(step == at)
        def _(at=at, part=part):
            term = dot_nt(part[...], weight_ref[...])
            if at == 0:
                total[...] = term + before_ref[...] if held else term
            else:
                total[...] += term

    @pl.when(step == count - 1)
    def _():
        out_ref[...] = total[...].astype(out_ref.dtype)


def feature_grad(order, parts, weight, before, last):
    rows, width = parts[0].shape
    features = weight.shape[0]
    count = len(parts)
    whole = lambda shape: pl.BlockSpec(shape, lambda i, order: (0, 0))
    return pl.pallas_call(
        functools.partial(feature_kernel, count=count, held=before is not None, last=last),
        out_shape=jax.ShapeDtypeStruct((rows, features), BF16 if last else F32),
        grid_spec=pltpu.PrefetchScalarGridSpec(
            num_scalar_prefetch=1,
            grid=(count,),
            in_specs=[whole((rows, width))] * count
            + [pl.BlockSpec((features, width), lambda i, order: (0, order[i]))]
            + ([whole((rows, features))] if before is not None else []),
            out_specs=whole((rows, features)),
            scratch_shapes=[pltpu.VMEM((rows, features), F32)],
        ),
        compiler_params=params(16),
        cost_estimate=cost(2 * rows * width * features * count, 2 * width * features * count),
        name="feature_grad",
    )(order, *parts, weight, *([before] if before is not None else []))


def flipped(count, flip):
    return [(i, i ^ flip) for i in range(count)]


def on_device(
    queries, text_kv, out_grad, text_segment, visual_rows, kv_weight, visual_dest, visual_sample
):
    groups, shares = lax.axis_size("group"), lax.axis_size("tensor")
    rows = visual_rows.shape[0]
    capacity = 2 * rows // groups
    width = kv_weight.shape[1] // shares
    here = lax.axis_index("tensor").astype(jnp.int32)
    me = lax.axis_index("group").astype(jnp.int32).reshape(1)
    dest_row = visual_dest.reshape(1, rows)
    sample_col = visual_sample.reshape(rows, 1)

    flips = list(range(shares - 1, 0, -1)) + [0]
    order = here ^ jnp.array(flips, jnp.int32)
    half = shares // 2
    blocks = project(order[:half], visual_rows, kv_weight, width, [BF16] * half)
    landed = [
        lax.ppermute(block, "tensor", flipped(shares, flip))
        for block, flip in zip(blocks, flips[:half], strict=True)
    ]
    near = project(
        order[half:], visual_rows, kv_weight, width, [BF16] * (shares - half - 1) + [F32]
    )
    landed += [
        lax.ppermute(block, "tensor", flipped(shares, flip))
        for block, flip in zip(near[:-1], flips[half:-1], strict=True)
    ]
    stats = text_stats(queries, out_grad, text_kv, text_segment)

    pairwise = groups == 8
    if pairwise:
        same = [2 * j for j in range(groups // 2)]
        other = [2 * j + 1 for j in range(groups // 2)]
        slots = [[flip] for flip in same] + [other]
        *mine, across = place(me, dest_row, sample_col, near[-1], landed, capacity, slots)
        theirs = lax.ppermute(across, "group", flipped(groups, 1))
        pairs = [
            jnp.concatenate([one, theirs[j * capacity : (j + 1) * capacity]], axis=0)
            for j, one in enumerate(mine)
        ]
        visual = [
            pair if flip == 0 else lax.ppermute(pair, "group", flipped(groups, flip))
            for pair, flip in zip(pairs, same, strict=True)
        ]
    else:
        slots = [list(range(groups))]
        (sent,) = place(me, dest_row, sample_col, near[-1], landed, capacity, slots)
        visual = [
            lax.all_to_all(
                sent.reshape(groups, capacity, -1), "group", split_axis=0, concat_axis=0, tiled=True
            ).reshape(groups * capacity, -1)
        ]

    grads, final = slot_grad(queries, out_grad, text_segment, stats, visual)
    attended, query_grad, text_kv_grad = text_grad(
        queries, out_grad, text_kv, text_segment, final, visual
    )

    if pairwise:
        back = [
            grad if flip == 0 else lax.ppermute(grad, "group", flipped(groups, flip))
            for grad, flip in zip(grads, same, strict=True)
        ]
        kept = jnp.concatenate([one[:capacity] for one in back], axis=0)
        passed = jnp.concatenate([one[capacity:] for one in back], axis=0)
        passed = lax.ppermute(passed, "group", flipped(groups, 1))
        returned, slots = [kept, passed], [same, other]
    else:
        returned = [
            lax.all_to_all(
                grads[0].reshape(groups, capacity, -1),
                "group",
                split_axis=0,
                concat_axis=0,
                tiled=True,
            ).reshape(groups * capacity, -1)
        ]
    kv_grad = collect(me, visual_dest, returned, capacity, slots)

    gathered = [
        lax.ppermute(kv_grad, "tensor", flipped(shares, flip)) for flip in flips[:-1]
    ] + [kv_grad]
    begun = feature_grad(order[half:][::-1], gathered[half:][::-1], kv_weight, None, False)
    visual_grad = feature_grad(order[:half], gathered[:half], kv_weight, begun, True)
    return (attended, query_grad, text_kv_grad, visual_grad)


def solution(mesh):
    placed = (
        P("group", "tensor"),
        P("group", "tensor"),
        P("group", "tensor"),
        P("group", None),
        P("group", "tensor"),
        P("tensor", None),
        P("group", None),
        P("group"),
    )
    return jax.shard_map(
        on_device,
        mesh=mesh,
        in_specs=placed,
        out_specs=(
            P("group", "tensor"),
            P("group", "tensor"),
            P("group", "tensor"),
            P("group", "tensor"),
        ),
        check_vma=False,
    )
```

```python
import functools
import math

import jax
import jax.numpy as jnp
from jax import lax
from jax.experimental import pallas as pl
from jax.experimental.pallas import tpu as pltpu
from jax.sharding import PartitionSpec as P

HD = 128
QPK = 4
TILE = 128
SCALE = 1.0 / math.sqrt(HD)
LOG2E = math.log2(math.e)
F32 = jnp.float32
BF16 = jnp.bfloat16
MIB = 1024 * 1024


def dot_nn(a, b):
    return lax.dot_general(a, b, (((1,), (0,)), ((), ())), preferred_element_type=F32)


def dot_nt(a, b):
    return lax.dot_general(a, b, (((1,), (1,)), ((), ())), preferred_element_type=F32)


def dot_tn(a, b):
    return lax.dot_general(a, b, (((0,), (0,)), ((), ())), preferred_element_type=F32)


def in_hbm(x):
    return pltpu.with_memory_space_constraint(x, pltpu.HBM)


def params(mib):
    return pltpu.CompilerParams(vmem_limit_bytes=mib * MIB)


def cost(flops, moved, exps=0):
    return pl.CostEstimate(flops=flops, bytes_accessed=moved, transcendentals=exps)


def project_kernel(rows_ref, weight_ref, *refs, turns, steps, held):
    count, refs = len(turns), refs[held:]
    outs, weights = refs[:count], refs[count : 2 * count]
    rows, rows_sem, weight_sems = refs[2 * count :]
    here, shares = lax.axis_index("tensor"), lax.axis_size("tensor")
    odd = lax.axis_index("group") & 1
    features, width = weights[0].shape
    depth = features // steps
    rows_copy = pltpu.make_async_copy(rows_ref, rows, rows_sem)
    rows_copy.start()
    copies = []
    for at, (even_turn, odd_turn) in enumerate(turns):
        turn = jnp.where(odd == 1, odd_turn, even_turn)
        first = pl.multiple_of(lax.rem(here + turn, shares) * width, width)
        for step in range(steps):
            part = pl.ds(step * depth, depth)
            copy = pltpu.make_async_copy(
                weight_ref.at[part, pl.ds(first, width)],
                weights[at].at[part],
                weight_sems.at[at, step],
            )
            copy.start()
            copies.append(copy)
    rows_copy.wait()
    for at, out in enumerate(outs):
        total = None
        for step in range(steps):
            copies[at * steps + step].wait()
            part = slice(step * depth, (step + 1) * depth)
            term = dot_nn(rows[:, part], weights[at][part, :])
            total = term if total is None else total + term
        out[...] = total.astype(out.dtype)


def project(rows, weight, after, width, turns, kinds):
    count, features = rows.shape
    steps = 4
    vmem, hbm = pl.BlockSpec(memory_space=pltpu.VMEM), pl.BlockSpec(memory_space=pltpu.HBM)
    found = pl.pallas_call(
        functools.partial(project_kernel, turns=turns, steps=steps, held=len(after)),
        out_shape=[jax.ShapeDtypeStruct((count, width), kind) for kind in kinds]
        + [jax.ShapeDtypeStruct((features, width), BF16) for _ in kinds],
        in_specs=[hbm, hbm] + [pl.BlockSpec(memory_space=pl.ANY)] * len(after),
        out_specs=[vmem] * (2 * len(kinds)),
        scratch_shapes=[
            pltpu.VMEM((count, features), BF16),
            pltpu.SemaphoreType.DMA,
            pltpu.SemaphoreType.DMA((len(kinds), steps)),
        ],
        compiler_params=params(16),
        cost_estimate=cost(
            2 * count * features * width * len(kinds), 2 * features * width * len(kinds)
        ),
        name="project",
    )(in_hbm(rows), in_hbm(weight), *after)
    return found[: len(kinds)], found[len(kinds) :]


FLIPS = ((2, 4), (4, 2), (6, 6), (0, 0))


def target_of(slot, capacity, across, flips):
    if across is None:
        return slot // capacity
    me = lax.axis_index("group") ^ across
    odd = me & 1
    target = jnp.zeros(slot.shape, jnp.int32)
    for at, (even_flip, odd_flip) in enumerate(flips):
        pack = me ^ jnp.where(odd == 1, odd_flip, even_flip)
        target = jnp.where(slot // capacity == at, pack, target)
    return target


def place_kernel(dest_ref, sample_ref, own_ref, *refs, capacity, plan):
    parts, outs = refs[: -len(plan)], refs[-len(plan) :]
    total = own_ref[...]
    for part in parts:
        total = total + part[...].astype(F32)
    tags = jnp.broadcast_to(sample_ref[...] + 1, (TILE, total.shape[0])).astype(F32).T
    wide = jnp.concatenate([total, tags], axis=1).astype(BF16)
    rows = total.shape[0]
    for out, across in zip(outs, plan, strict=True):
        slots = out.shape[0]
        slot = lax.broadcasted_iota(jnp.int32, (slots, rows), 0)
        row = lax.broadcasted_iota(jnp.int32, (slots, rows), 1)
        target = target_of(slot, capacity, across, FLIPS)
        select = (dest_ref[...] == target) & (slot % capacity == row % capacity)
        out[...] = dot_nn(select.astype(F32).astype(BF16), wide).astype(BF16)


def place(dest_row, sample_row, own, parts, capacity, slots, plan):
    rows, width = own.shape
    vmem = pl.BlockSpec(memory_space=pltpu.VMEM)
    return pl.pallas_call(
        functools.partial(place_kernel, capacity=capacity, plan=plan),
        out_shape=[jax.ShapeDtypeStruct((slots, width + TILE), BF16) for _ in plan],
        in_specs=[vmem] * (3 + len(parts)),
        out_specs=[vmem] * len(plan),
        compiler_params=params(8),
        cost_estimate=cost(2 * 256 * rows * width, 4 * rows * width),
        name="place",
    )(dest_row, sample_row, own, *parts)


def collect_kernel(dest_ref, *refs, capacity, plan):
    parts, out = refs[:-1], refs[-1]
    rows = out.shape[0]
    total = jnp.zeros(out.shape, F32)
    for part, across in zip(parts, plan, strict=True):
        slots = part.shape[0]
        slot = lax.broadcasted_iota(jnp.int32, (rows, slots), 1)
        row = lax.broadcasted_iota(jnp.int32, (rows, slots), 0)
        target = target_of(slot, capacity, across, FLIPS[::-1])
        dest = jnp.broadcast_to(dest_ref[...], (slots, rows)).astype(F32).T
        select = (dest == target.astype(F32)) & (slot % capacity == row % capacity)
        total = total + dot_nn(select.astype(F32).astype(BF16), part[...])
    out[...] = total.astype(BF16)


def collect(dest_row, parts, capacity, plan):
    rows, width = dest_row.shape[1], parts[0].shape[1]
    vmem = pl.BlockSpec(memory_space=pltpu.VMEM)
    return pl.pallas_call(
        functools.partial(collect_kernel, capacity=capacity, plan=plan),
        out_shape=jax.ShapeDtypeStruct((rows, width), BF16),
        in_specs=[vmem] * (1 + len(parts)),
        out_specs=vmem,
        compiler_params=params(8),
        cost_estimate=cost(2 * 256 * rows * width, 4 * rows * width),
        name="collect",
    )(dest_row, *parts)


def stacked(ref, tile, head):
    first = head * QPK * HD
    return jnp.concatenate(
        [
            ref[tile * TILE : (tile + 1) * TILE, first + j * HD : first + (j + 1) * HD]
            for j in range(QPK)
        ],
        axis=0,
    )


def text_span(tile):
    return max(0, tile - 1) * TILE, (tile + 1) * TILE


def text_mask(segment_ref, tile):
    low, high = text_span(tile)
    span = high - low
    own = segment_ref[:, tile * TILE : (tile + 1) * TILE].astype(F32)
    keys = jnp.concatenate(
        [
            jnp.broadcast_to(segment_ref[:, at : at + TILE].astype(F32), (TILE, TILE)).T
            for at in range(low, high, TILE)
        ],
        axis=0,
    )
    key_place = lax.broadcasted_iota(jnp.int32, (span, TILE), 0) + low
    token_place = lax.broadcasted_iota(jnp.int32, (span, TILE), 1) + tile * TILE
    mask = (keys == own) & (key_place <= token_place)
    return jnp.where(mask, 0.0, -jnp.inf)


def slot_mask(tags, segment_ref, tile):
    own = segment_ref[:, tile * TILE : (tile + 1) * TILE].astype(F32) + 1.0
    return jnp.where(tags.astype(F32) == own, 0.0, -jnp.inf)


def repeated(mask):
    return jnp.concatenate([mask] * QPK, axis=1)


def text_stats_kernel(query_ref, grad_ref, kv_ref, segment_ref, top_ref, sum_ref, inner_ref):
    tiles, heads = query_ref.shape[0] // TILE, kv_ref.shape[1] // (2 * HD)
    for tile in range(tiles):
        low, high = text_span(tile)
        mask = repeated(text_mask(segment_ref, tile))
        for head in range(heads):
            at = head * tiles + tile
            keys = kv_ref[low:high, head * 2 * HD : head * 2 * HD + HD]
            values = kv_ref[low:high, head * 2 * HD + HD : (head + 1) * 2 * HD]
            scores = dot_nt(keys, stacked(query_ref, tile, head)) + mask
            top = jnp.max(scores, axis=0, keepdims=True)
            expo = jnp.exp2((scores - top) * (SCALE * LOG2E))
            dprobs = dot_nt(values, stacked(grad_ref, tile, head))
            top_ref[at : at + 1, :] = top
            sum_ref[at : at + 1, :] = jnp.sum(expo, axis=0, keepdims=True)
            inner_ref[at : at + 1, :] = jnp.sum(expo * dprobs, axis=0, keepdims=True)


def text_stats(queries, out_grad, text_kv, segment):
    tiles, heads = queries.shape[0] // TILE, text_kv.shape[1] // (2 * HD)
    vmem = pl.BlockSpec(memory_space=pltpu.VMEM)
    shape = jax.ShapeDtypeStruct((tiles * heads, QPK * TILE), F32)
    pairs = heads * QPK * (2 * tiles - 1) * TILE * TILE
    return pl.pallas_call(
        text_stats_kernel,
        out_shape=[shape] * 3,
        in_specs=[vmem] * 4,
        out_specs=[vmem] * 3,
        compiler_params=params(24),
        cost_estimate=cost(4 * pairs * HD, 4 * queries.size, pairs),
        name="text_stats",
    )(queries, out_grad, text_kv, segment)


def slot_grad_kernel(
    query_ref, grad_ref, segment_ref, top_ref, sum_ref, inner_ref, *refs, arrivals
):
    visual, refs = refs[:arrivals], refs[arrivals:]
    outs, (all_top_ref, scale_ref, all_inner_ref) = refs[:arrivals], refs[arrivals:]
    tiles = query_ref.shape[0] // TILE
    width = visual[0].shape[1] - TILE
    heads = width // (2 * HD)
    tags = jnp.concatenate([one[:, width:] for one in visual], axis=0)
    masks = [slot_mask(tags, segment_ref, tile) for tile in range(tiles)]
    for head in range(heads):
        first = head * 2 * HD
        keys = jnp.concatenate([one[:, first : first + HD] for one in visual], axis=0)
        values = jnp.concatenate([one[:, first + HD : first + 2 * HD] for one in visual], axis=0)
        key_grad = jnp.zeros((keys.shape[0], HD), F32)
        value_grad = jnp.zeros((keys.shape[0], HD), F32)
        for tile in range(tiles):
            at = head * tiles + tile
            query, grad = stacked(query_ref, tile, head), stacked(grad_ref, tile, head)
            scores = dot_nt(keys, query) + repeated(masks[tile])
            dprobs = dot_nt(values, grad)
            text_top = top_ref[at : at + 1, :]
            top = jnp.maximum(text_top, jnp.max(scores, axis=0, keepdims=True))
            expo = jnp.exp2((scores - top) * (SCALE * LOG2E))
            shift = jnp.exp2((text_top - top) * (SCALE * LOG2E))
            total = sum_ref[at : at + 1, :] * shift + jnp.sum(expo, axis=0, keepdims=True)
            inverse = 1.0 / total
            inner = (
                inner_ref[at : at + 1, :] * shift + jnp.sum(expo * dprobs, axis=0, keepdims=True)
            ) * inverse
            probs = expo * inverse
            dscores = (probs * (dprobs - inner)).astype(BF16)
            value_grad = value_grad + dot_nn(probs.astype(BF16), grad)
            key_grad = key_grad + dot_nn(dscores, query)
            all_top_ref[at : at + 1, :] = top
            scale_ref[at : at + 1, :] = inverse
            all_inner_ref[at : at + 1, :] = inner
        for at, out in enumerate(outs[::-1]):
            rows = slice(at * out.shape[0], (at + 1) * out.shape[0])
            out[:, first : first + HD] = (key_grad[rows] * SCALE).astype(BF16)
            out[:, first + HD : first + 2 * HD] = value_grad[rows].astype(BF16)


def slot_grad(queries, out_grad, segment, stats, visual):
    vmem = pl.BlockSpec(memory_space=pltpu.VMEM)
    shape = jax.ShapeDtypeStruct(stats[0].shape, F32)
    slots = sum(one.shape[0] for one in visual)
    pairs = slots * queries.shape[0] * queries.shape[1] // HD
    found = pl.pallas_call(
        functools.partial(slot_grad_kernel, arrivals=len(visual)),
        out_shape=[
            jax.ShapeDtypeStruct((one.shape[0], one.shape[1] - TILE), BF16) for one in visual
        ]
        + [shape] * 3,
        in_specs=[vmem] * (6 + len(visual)),
        out_specs=[vmem] * (3 + len(visual)),
        compiler_params=params(24),
        cost_estimate=cost(8 * pairs * HD, 4 * queries.size, pairs),
        name="slot_grad",
    )(queries, out_grad, segment, *stats, *visual)
    return found[: len(visual)][::-1], found[len(visual) :]


def text_grad_kernel(
    query_ref,
    grad_ref,
    kv_ref,
    segment_ref,
    top_ref,
    scale_ref,
    inner_ref,
    *refs,
    arrivals,
    head,
    held,
):
    visual, refs = refs[:arrivals], refs[arrivals + held :]
    outs, (attended_all, query_grad_all, kv_grad_all, sems) = refs[:3], refs[3:]
    tiles, width = query_ref.shape[0] // TILE, kv_ref.shape[1]
    first = head * 2 * HD
    tags = jnp.concatenate([one[:, width:] for one in visual], axis=0)
    slot_keys = jnp.concatenate([one[:, first : first + HD] for one in visual], axis=0)
    slot_values = jnp.concatenate([one[:, first + HD : first + 2 * HD] for one in visual], axis=0)
    key_held = value_held = None
    copies = []

    def send(which, held, rows, start):
        copy = pltpu.make_async_copy(
            held.at[rows],
            outs[which].at[rows, start : start + held.shape[1]],
            sems.at[len(copies)],
        )
        copy.start()
        copies.append(copy)

    for tile in range(tiles):
        at = head * tiles + tile
        low, high = text_span(tile)
        mask = repeated(
            jnp.concatenate(
                [text_mask(segment_ref, tile), slot_mask(tags, segment_ref, tile)], axis=0
            )
        )
        keys = jnp.concatenate([kv_ref[low:high, first : first + HD], slot_keys], axis=0)
        values = jnp.concatenate(
            [kv_ref[low:high, first + HD : first + 2 * HD], slot_values], axis=0
        )
        query, grad = stacked(query_ref, tile, head), stacked(grad_ref, tile, head)
        scores = dot_nt(keys, query) + mask
        expo = jnp.exp2((scores - top_ref[at : at + 1, :]) * (SCALE * LOG2E))
        probs = expo * scale_ref[at : at + 1, :]
        dprobs = dot_nt(values, grad)
        dscores = (probs * (dprobs - inner_ref[at : at + 1, :])).astype(BF16)
        weights = probs.astype(BF16)
        attended = dot_tn(values, weights)
        query_grad = dot_tn(keys, dscores) * SCALE
        rows = slice(tile * TILE, (tile + 1) * TILE)
        for j in range(QPK):
            lanes = slice(j * TILE, (j + 1) * TILE)
            columns = slice(j * HD, (j + 1) * HD)
            attended_all[rows, columns] = attended[:, lanes].T.astype(BF16)
            query_grad_all[rows, columns] = query_grad[:, lanes].T.astype(BF16)
        send(0, attended_all, rows, head * QPK * HD)
        send(1, query_grad_all, rows, head * QPK * HD)
        key_part = dot_nn(dscores[: high - low], query)
        value_part = dot_nn(weights[: high - low], grad)
        if tile > 0:
            before = slice((tile - 1) * TILE, tile * TILE)
            kv_grad_all[before, :HD] = ((key_held + key_part[:TILE]) * SCALE).astype(BF16)
            kv_grad_all[before, HD:] = (value_held + value_part[:TILE]).astype(BF16)
            send(2, kv_grad_all, before, first)
        key_held, value_held = key_part[high - low - TILE :], value_part[high - low - TILE :]
    last = slice((tiles - 1) * TILE, tiles * TILE)
    kv_grad_all[last, :HD] = (key_held * SCALE).astype(BF16)
    kv_grad_all[last, HD:] = value_held.astype(BF16)
    send(2, kv_grad_all, last, first)
    for copy in copies:
        copy.wait()


def text_grad(queries, out_grad, text_kv, segment, stats, visual, head, before):
    vmem, hbm = pl.BlockSpec(memory_space=pltpu.VMEM), pl.BlockSpec(memory_space=pltpu.HBM)
    length = queries.shape[0]
    slots = sum(one.shape[0] for one in visual)
    pairs = (slots + 2 * TILE) * length * QPK
    first = 7 + len(visual)
    return pl.pallas_call(
        functools.partial(
            text_grad_kernel, arrivals=len(visual), head=head, held=len(before)
        ),
        out_shape=[
            jax.ShapeDtypeStruct(queries.shape, BF16),
            jax.ShapeDtypeStruct(queries.shape, BF16),
            jax.ShapeDtypeStruct(text_kv.shape, BF16),
        ],
        in_specs=[vmem] * first + [hbm] * len(before),
        out_specs=[hbm] * 3,
        scratch_shapes=[
            pltpu.VMEM((length, QPK * HD), BF16),
            pltpu.VMEM((length, QPK * HD), BF16),
            pltpu.VMEM((length, 2 * HD), BF16),
            pltpu.SemaphoreType.DMA((3 * length // TILE,)),
        ],
        input_output_aliases={first + i: i for i in range(len(before))},
        compiler_params=params(24),
        cost_estimate=cost(12 * pairs * HD, 8 * queries.size, pairs),
        name="text_grad",
    )(queries, out_grad, text_kv, segment, *stats, *visual, *before)


def near_kernel(*refs, count):
    total = None
    for part, weight in zip(refs[:count], refs[count : 2 * count], strict=True):
        term = dot_nt(part[...], weight[...])
        total = term if total is None else total + term
    refs[-1][...] = total


def near_grad(parts, weights):
    rows, (features, width) = parts[0].shape[0], weights[0].shape
    vmem = pl.BlockSpec(memory_space=pltpu.VMEM)
    return pl.pallas_call(
        functools.partial(near_kernel, count=len(parts)),
        out_shape=jax.ShapeDtypeStruct((rows, features), F32),
        in_specs=[vmem] * (2 * len(parts)),
        out_specs=vmem,
        compiler_params=params(16),
        cost_estimate=cost(
            2 * rows * width * features * len(parts), 2 * width * features * len(parts)
        ),
        name="near_grad",
    )(*parts, *weights)


def far_kernel(part_ref, weight_ref, before_ref, out_ref):
    out_ref[...] = before_ref[...] + dot_nt(part_ref[...], weight_ref[...])


def far_grad(part, weight, before):
    rows, width = part.shape
    features = weight.shape[0]
    vmem = pl.BlockSpec(memory_space=pltpu.VMEM)
    return pl.pallas_call(
        far_kernel,
        out_shape=jax.ShapeDtypeStruct((rows, features), F32),
        in_specs=[vmem] * 3,
        out_specs=vmem,
        compiler_params=params(16),
        cost_estimate=cost(2 * rows * width * features, 2 * width * features),
        name="far_grad",
    )(part, weight, before)


def last_kernel(part_ref, weight_ref, before_ref, out_ref, rounded, sems):
    steps = sems.shape[0]
    count = out_ref.shape[1] // steps
    copies = []
    for step in range(steps):
        columns = slice(step * count, (step + 1) * count)
        term = dot_nt(part_ref[...], weight_ref[columns, :])
        rounded[:, columns] = (before_ref[:, columns] + term).astype(BF16)
        copies.append(
            pltpu.make_async_copy(
                rounded.at[:, columns], out_ref.at[:, columns], sems.at[step]
            )
        )
        copies[-1].start()
    for copy in copies:
        copy.wait()


def last_grad(part, weight, before):
    rows, width = part.shape
    features = weight.shape[0]
    vmem, hbm = pl.BlockSpec(memory_space=pltpu.VMEM), pl.BlockSpec(memory_space=pltpu.HBM)
    return pl.pallas_call(
        last_kernel,
        out_shape=jax.ShapeDtypeStruct((rows, features), BF16),
        in_specs=[vmem] * 3,
        out_specs=hbm,
        scratch_shapes=[pltpu.VMEM((rows, features), BF16), pltpu.SemaphoreType.DMA((4,))],
        compiler_params=params(16),
        cost_estimate=cost(2 * rows * width * features, 2 * width * features),
        name="last_grad",
    )(part, weight, before)


def turned(groups, shares, turns, sign):
    return [
        (g * shares + t, g * shares + (t + sign * turns[g % 2]) % shares)
        for g in range(groups)
        for t in range(shares)
    ]


def on_device(
    queries, text_kv, out_grad, text_segment, visual_rows, kv_weight, visual_dest, visual_sample
):
    groups, shares = lax.axis_size("group"), lax.axis_size("tensor")
    rows = visual_rows.shape[0]
    capacity = 2 * rows // groups
    width = kv_weight.shape[1] // shares
    dest_row = visual_dest.reshape(1, rows)
    sample_row = visual_sample.reshape(1, rows)

    around = list(range(1, shares))
    turns = list(zip(around, around[1:] + around[:1], strict=True))
    axes = ("group", "tensor")
    landed, columns = [], []
    for batch in (turns[: shares // 2], turns[shares // 2 :]):
        blocks, weights = project(visual_rows, kv_weight, (), width, batch, [BF16] * len(batch))
        landed += [
            lax.ppermute(block, axes, turned(groups, shares, turn, 1))
            for block, turn in zip(blocks, batch, strict=True)
        ]
        columns += weights
    (own,), (own_columns,) = project(
        visual_rows, kv_weight, blocks[-1:], width, [(0, 0)], [F32]
    )
    stats = text_stats(queries, out_grad, text_kv, text_segment)

    pairwise = groups == 8
    if pairwise:
        ways = [
            [(g, g ^ (odd_flip if g % 2 else even_flip)) for g in range(groups)]
            for even_flip, odd_flip in FLIPS
        ]
        neighbour = [(g, g ^ 1) for g in range(groups)]
        plan = [0, 1]
        mine, across = place(
            dest_row, sample_row, own, landed, capacity, len(FLIPS) * capacity, plan
        )
        theirs = lax.ppermute(across, "group", neighbour)
        pairs = [
            jnp.concatenate(
                [mine[j * capacity : (j + 1) * capacity], theirs[j * capacity : (j + 1) * capacity]],
                axis=0,
            )
            for j in range(len(FLIPS))
        ]
        visual = [lax.ppermute(pair, "group", way) for pair, way in zip(pairs[:-1], ways[:-1])]
        visual.append(pairs[-1])
    else:
        plan = [None]
        (sent,) = place(
            dest_row, sample_row, own, landed, capacity, groups * capacity, plan
        )
        visual = [
            lax.all_to_all(
                sent.reshape(groups, capacity, -1), "group", split_axis=0, concat_axis=0, tiled=True
            ).reshape(groups * capacity, -1)
        ]

    grads, final = slot_grad(queries, out_grad, text_segment, stats, visual)
    inputs = (queries, out_grad, text_kv, text_segment, final, visual)
    text_outs = text_grad(*inputs, 0, ())

    if pairwise:
        back = [lax.ppermute(grad, "group", way) for grad, way in zip(grads[:-1], ways[:-1])]
        back = [grads[-1]] + back[::-1]
        *back, kept = lax.optimization_barrier((*back, text_outs[2]))
        text_outs = (*text_outs[:2], kept)
        kept = jnp.concatenate([one[:capacity] for one in back], axis=0)
        passed = jnp.concatenate([one[capacity:] for one in back], axis=0)
        returned = [kept, lax.ppermute(passed, "group", neighbour)]
    else:
        returned = [
            lax.all_to_all(
                grads[0].reshape(groups, capacity, -1),
                "group",
                split_axis=0,
                concat_axis=0,
                tiled=True,
            ).reshape(groups * capacity, -1)
        ]
    kv_grad = collect(dest_row, returned, capacity, plan)

    for head in range(1, text_kv.shape[1] // (2 * HD)):
        text_outs = text_grad(*inputs, head, text_outs)
    attended, query_grad, text_kv_grad = text_outs

    gathered = [
        lax.ppermute(kv_grad, axes, turned(groups, shares, turn, -1)) for turn in turns
    ]
    total = near_grad([kv_grad, gathered[0]], [own_columns, columns[0]])
    for part, weight in zip(gathered[2:], columns[2:], strict=True):
        total = far_grad(part, weight, total)
    total = last_grad(gathered[1], columns[1], total)
    return (attended, query_grad, text_kv_grad, total)


def solution(mesh):
    placed = (
        P("group", "tensor"),
        P("group", "tensor"),
        P("group", "tensor"),
        P("group", None),
        P("group", "tensor"),
        P("tensor", None),
        P("group", None),
        P("group"),
    )
    return jax.shard_map(
        on_device,
        mesh=mesh,
        in_specs=placed,
        out_specs=(
            P("group", "tensor"),
            P("group", "tensor"),
            P("group", "tensor"),
            P("group", "tensor"),
        ),
        check_vma=False,
    )
```

```python
import functools
import math

import jax
import jax.numpy as jnp
from jax import lax
from jax.experimental import pallas as pl
from jax.experimental.pallas import tpu as pltpu
from jax.sharding import PartitionSpec as P

HD = 128
QPK = 4
TILE = 128
SCALE = 1.0 / math.sqrt(HD)
LOG2E = math.log2(math.e)
F32 = jnp.float32
BF16 = jnp.bfloat16
MIB = 1024 * 1024


def dot_nn(a, b):
    return lax.dot_general(a, b, (((1,), (0,)), ((), ())), preferred_element_type=F32)


def dot_nt(a, b):
    return lax.dot_general(a, b, (((1,), (1,)), ((), ())), preferred_element_type=F32)


def dot_tn(a, b):
    return lax.dot_general(a, b, (((0,), (0,)), ((), ())), preferred_element_type=F32)


def in_hbm(x):
    return pltpu.with_memory_space_constraint(x, pltpu.HBM)


def params(mib):
    return pltpu.CompilerParams(vmem_limit_bytes=mib * MIB)


def cost(flops, moved, exps=0):
    return pl.CostEstimate(flops=flops, bytes_accessed=moved, transcendentals=exps)


def project_kernel(rows_ref, weight_ref, *refs, flips, steps, held):
    count, refs = len(flips), refs[held:]
    outs, weights = refs[:count], refs[count : 2 * count]
    rows, rows_sem, weight_sems = refs[2 * count :]
    here = lax.axis_index("tensor")
    features, width = weights[0].shape
    depth = features // steps
    rows_copy = pltpu.make_async_copy(rows_ref, rows, rows_sem)
    rows_copy.start()
    copies = []
    for at, flip in enumerate(flips):
        first = pl.multiple_of((here ^ flip) * width, width)
        for step in range(steps):
            part = pl.ds(step * depth, depth)
            copy = pltpu.make_async_copy(
                weight_ref.at[part, pl.ds(first, width)],
                weights[at].at[part],
                weight_sems.at[at, step],
            )
            copy.start()
            copies.append(copy)
    rows_copy.wait()
    for at, out in enumerate(outs):
        total = None
        for step in range(steps):
            copies[at * steps + step].wait()
            part = slice(step * depth, (step + 1) * depth)
            term = dot_nn(rows[:, part], weights[at][part, :])
            total = term if total is None else total + term
        out[...] = total.astype(out.dtype)


def project(rows, weight, after, width, flips, kinds):
    count, features = rows.shape
    steps = 4
    vmem, hbm = pl.BlockSpec(memory_space=pltpu.VMEM), pl.BlockSpec(memory_space=pltpu.HBM)
    found = pl.pallas_call(
        functools.partial(project_kernel, flips=flips, steps=steps, held=len(after)),
        out_shape=[jax.ShapeDtypeStruct((count, width), kind) for kind in kinds]
        + [jax.ShapeDtypeStruct((features, width), BF16) for _ in kinds],
        in_specs=[hbm, hbm] + [pl.BlockSpec(memory_space=pl.ANY)] * len(after),
        out_specs=[vmem] * (2 * len(kinds)),
        scratch_shapes=[
            pltpu.VMEM((count, features), BF16),
            pltpu.SemaphoreType.DMA,
            pltpu.SemaphoreType.DMA((len(kinds), steps)),
        ],
        compiler_params=params(16),
        cost_estimate=cost(
            2 * count * features * width * len(kinds), 2 * features * width * len(kinds)
        ),
        name="project",
    )(in_hbm(rows), in_hbm(weight), *after)
    return found[: len(kinds)], found[len(kinds) :]


FLIPS = ((6, 6), (4, 2), (2, 4), (0, 0))
BACK = (0, 2, 1)


def target_of(slot, capacity, flips):
    if flips is None:
        return slot // capacity
    me = lax.axis_index("group")
    odd = me & 1
    chip = jnp.zeros(slot.shape, jnp.int32)
    for at, (even_flip, odd_flip) in enumerate(flips):
        pack = me ^ jnp.where(odd == 1, odd_flip, even_flip)
        chip = jnp.where(slot // (2 * capacity) == at, pack, chip)
    return chip ^ ((slot // capacity) & 1)


def place_kernel(dest_ref, sample_ref, own_ref, *refs, capacity, flips, count):
    parts, outs = refs[:-count], refs[-count:]
    total = own_ref[...]
    for part in parts:
        total = total + part[...].astype(F32)
    rows = total.shape[0]
    tags = jnp.broadcast_to(sample_ref[...] + 1, (TILE, rows)).astype(F32).T
    wide = jnp.concatenate([total, tags], axis=1).astype(BF16)
    each = outs[0].shape[0]
    slot = lax.broadcasted_iota(jnp.int32, (each * count, rows), 0)
    row = lax.broadcasted_iota(jnp.int32, (each * count, rows), 1)
    target = target_of(slot, capacity, flips)
    select = (dest_ref[...] == target) & (slot % capacity == row % capacity)
    placed = dot_nn(select.astype(F32).astype(BF16), wide).astype(BF16)
    for at, out in enumerate(outs):
        out[...] = placed[at * each : (at + 1) * each]


def place(dest_row, sample_row, own, parts, capacity, slots, flips):
    rows, width = own.shape
    count = len(flips) if flips else 1
    vmem = pl.BlockSpec(memory_space=pltpu.VMEM)
    return pl.pallas_call(
        functools.partial(place_kernel, capacity=capacity, flips=flips, count=count),
        out_shape=[jax.ShapeDtypeStruct((slots // count, width + TILE), BF16)] * count,
        in_specs=[vmem] * (3 + len(parts)),
        out_specs=[vmem] * count,
        compiler_params=params(8),
        cost_estimate=cost(2 * slots * rows * width, 4 * rows * width),
        name="place",
    )(dest_row, sample_row, own, *parts)


def collect_kernel(dest_ref, *refs, capacity, flips):
    parts, out = refs[:-1], refs[-1]
    rows = out.shape[0]
    grads = jnp.concatenate([part[...] for part in parts], axis=0)
    slots = grads.shape[0]
    slot = lax.broadcasted_iota(jnp.int32, (rows, slots), 1)
    row = lax.broadcasted_iota(jnp.int32, (rows, slots), 0)
    target = target_of(slot, capacity, flips)
    dest = jnp.broadcast_to(dest_ref[...], (slots, rows)).astype(F32).T
    select = (dest == target.astype(F32)) & (slot % capacity == row % capacity)
    out[...] = dot_nn(select.astype(F32).astype(BF16), grads).astype(BF16)


def collect(dest_row, parts, capacity, flips):
    rows, width = dest_row.shape[1], parts[0].shape[1]
    vmem = pl.BlockSpec(memory_space=pltpu.VMEM)
    return pl.pallas_call(
        functools.partial(collect_kernel, capacity=capacity, flips=flips),
        out_shape=jax.ShapeDtypeStruct((rows, width), BF16),
        in_specs=[vmem] * (1 + len(parts)),
        out_specs=vmem,
        compiler_params=params(8),
        cost_estimate=cost(2 * 256 * rows * width, 4 * rows * width),
        name="collect",
    )(dest_row, *parts)


def stacked(ref, tile, head):
    first = head * QPK * HD
    return jnp.concatenate(
        [
            ref[tile * TILE : (tile + 1) * TILE, first + j * HD : first + (j + 1) * HD]
            for j in range(QPK)
        ],
        axis=0,
    )


def text_span(tile):
    return max(0, tile - 1) * TILE, (tile + 1) * TILE


def text_mask(segment_ref, tile):
    low, high = text_span(tile)
    span = high - low
    own = segment_ref[:, tile * TILE : (tile + 1) * TILE].astype(F32)
    keys = jnp.concatenate(
        [
            jnp.broadcast_to(segment_ref[:, at : at + TILE].astype(F32), (TILE, TILE)).T
            for at in range(low, high, TILE)
        ],
        axis=0,
    )
    key_place = lax.broadcasted_iota(jnp.int32, (span, TILE), 0) + low
    token_place = lax.broadcasted_iota(jnp.int32, (span, TILE), 1) + tile * TILE
    mask = (keys == own) & (key_place <= token_place)
    return jnp.where(mask, 0.0, -jnp.inf)


def slot_mask(tags, segment_ref, tile):
    own = segment_ref[:, tile * TILE : (tile + 1) * TILE].astype(F32) + 1.0
    return jnp.where(tags.astype(F32) == own, 0.0, -jnp.inf)


def repeated(mask):
    return jnp.concatenate([mask] * QPK, axis=1)


def text_stats_kernel(query_ref, grad_ref, kv_ref, segment_ref, top_ref, sum_ref, inner_ref):
    tiles, heads = query_ref.shape[0] // TILE, kv_ref.shape[1] // (2 * HD)
    for tile in range(tiles):
        low, high = text_span(tile)
        mask = repeated(text_mask(segment_ref, tile))
        for head in range(heads):
            at = head * tiles + tile
            keys = kv_ref[low:high, head * 2 * HD : head * 2 * HD + HD]
            values = kv_ref[low:high, head * 2 * HD + HD : (head + 1) * 2 * HD]
            scores = dot_nt(keys, stacked(query_ref, tile, head)) + mask
            top = jnp.max(scores, axis=0, keepdims=True)
            expo = jnp.exp2((scores - top) * (SCALE * LOG2E))
            dprobs = dot_nt(values, stacked(grad_ref, tile, head))
            top_ref[at : at + 1, :] = top
            sum_ref[at : at + 1, :] = jnp.sum(expo, axis=0, keepdims=True)
            inner_ref[at : at + 1, :] = jnp.sum(expo * dprobs, axis=0, keepdims=True)


def text_stats(queries, out_grad, text_kv, segment):
    tiles, heads = queries.shape[0] // TILE, text_kv.shape[1] // (2 * HD)
    vmem = pl.BlockSpec(memory_space=pltpu.VMEM)
    shape = jax.ShapeDtypeStruct((tiles * heads, QPK * TILE), F32)
    pairs = heads * QPK * (2 * tiles - 1) * TILE * TILE
    return pl.pallas_call(
        text_stats_kernel,
        out_shape=[shape] * 3,
        in_specs=[vmem] * 4,
        out_specs=[vmem] * 3,
        compiler_params=params(24),
        cost_estimate=cost(4 * pairs * HD, 4 * queries.size, pairs),
        name="text_stats",
    )(queries, out_grad, text_kv, segment)


def slot_tiles(query_ref, grad_ref, segment_ref, slots_ref):
    tiles = query_ref.shape[0] // TILE
    width = slots_ref.shape[1] - TILE
    masks = [
        repeated(slot_mask(slots_ref[:, width:], segment_ref, tile)) for tile in range(tiles)
    ]
    for head in range(width // (2 * HD)):
        first = head * 2 * HD
        keys = slots_ref[:, first : first + HD]
        values = slots_ref[:, first + HD : first + 2 * HD]
        for tile in range(tiles):
            query, grad = stacked(query_ref, tile, head), stacked(grad_ref, tile, head)
            scores = dot_nt(keys, query) + masks[tile]
            yield head, tile, head * tiles + tile, query, grad, scores, dot_nt(values, grad)


def joined(scores, dprobs, top_ref, sum_ref, inner_ref, at):
    before = top_ref[at : at + 1, :]
    top = jnp.maximum(before, jnp.max(scores, axis=0, keepdims=True))
    expo = jnp.exp2((scores - top) * (SCALE * LOG2E))
    shift = jnp.exp2((before - top) * (SCALE * LOG2E))
    total = sum_ref[at : at + 1, :] * shift + jnp.sum(expo, axis=0, keepdims=True)
    inner = inner_ref[at : at + 1, :] * shift + jnp.sum(expo * dprobs, axis=0, keepdims=True)
    return expo, top, total, inner


def slot_stats_kernel(
    query_ref, grad_ref, segment_ref, slots_ref, top_ref, sum_ref, inner_ref, *outs
):
    for _, _, at, _, _, scores, dprobs in slot_tiles(query_ref, grad_ref, segment_ref, slots_ref):
        found = joined(scores, dprobs, top_ref, sum_ref, inner_ref, at)
        for out, row in zip(outs, found[1:], strict=True):
            out[at : at + 1, :] = row


def slot_grad_kernel(
    query_ref, grad_ref, segment_ref, slots_ref, top_ref, sum_ref, inner_ref, out_ref, *outs
):
    tiles, slots = query_ref.shape[0] // TILE, slots_ref.shape[0]
    for head, tile, at, query, grad, scores, dprobs in slot_tiles(
        query_ref, grad_ref, segment_ref, slots_ref
    ):
        if outs:
            expo, top, total, inner = joined(scores, dprobs, top_ref, sum_ref, inner_ref, at)
            inverse = 1.0 / total
            inner = inner * inverse
            for out, row in zip(outs, (top, inverse, inner), strict=True):
                out[at : at + 1, :] = row
        else:
            expo = jnp.exp2((scores - top_ref[at : at + 1, :]) * (SCALE * LOG2E))
            inverse, inner = sum_ref[at : at + 1, :], inner_ref[at : at + 1, :]
        probs = expo * inverse
        dscores = (probs * (dprobs - inner)).astype(BF16)
        value_part = dot_nn(probs.astype(BF16), grad)
        key_part = dot_nn(dscores, query)
        value_grad = value_part if tile == 0 else value_grad + value_part
        key_grad = key_part if tile == 0 else key_grad + key_part
        if tile == tiles - 1:
            first = head * 2 * HD
            out_ref[:, first : first + HD] = (key_grad * SCALE).astype(BF16)
            out_ref[:, first + HD : first + 2 * HD] = value_grad.astype(BF16)


def slot_call(kernel, queries, out_grad, segment, slots, stats, grads, joins, name):
    vmem = pl.BlockSpec(memory_space=pltpu.VMEM)
    pairs = slots.shape[0] * queries.shape[0] * queries.shape[1] // HD
    shapes = []
    if grads:
        shapes.append(jax.ShapeDtypeStruct((slots.shape[0], slots.shape[1] - TILE), BF16))
    if joins:
        shapes += [jax.ShapeDtypeStruct(stats[0].shape, F32)] * 3
    return pl.pallas_call(
        kernel,
        out_shape=shapes,
        in_specs=[vmem] * 7,
        out_specs=[vmem] * len(shapes),
        compiler_params=params(24),
        cost_estimate=cost((8 if grads else 4) * pairs * HD, 4 * queries.size, pairs),
        name=name,
    )(queries, out_grad, segment, slots, *stats)


def text_grad_kernel(
    query_ref,
    grad_ref,
    kv_ref,
    segment_ref,
    top_ref,
    scale_ref,
    inner_ref,
    *refs,
    arrivals,
    head,
    held,
):
    visual, refs = refs[:arrivals], refs[arrivals + held :]
    outs, (attended_all, query_grad_all, kv_grad_all, sems) = refs[:3], refs[3:]
    tiles, width = query_ref.shape[0] // TILE, kv_ref.shape[1]
    first = head * 2 * HD
    tags = jnp.concatenate([one[:, width:] for one in visual], axis=0)
    slot_keys = jnp.concatenate([one[:, first : first + HD] for one in visual], axis=0)
    slot_values = jnp.concatenate([one[:, first + HD : first + 2 * HD] for one in visual], axis=0)
    key_held = value_held = None
    copies = []

    def send(which, held, rows, start):
        copy = pltpu.make_async_copy(
            held.at[rows],
            outs[which].at[rows, start : start + held.shape[1]],
            sems.at[len(copies)],
        )
        copy.start()
        copies.append(copy)

    for tile in range(tiles):
        at = head * tiles + tile
        low, high = text_span(tile)
        mask = repeated(
            jnp.concatenate(
                [text_mask(segment_ref, tile), slot_mask(tags, segment_ref, tile)], axis=0
            )
        )
        keys = jnp.concatenate([kv_ref[low:high, first : first + HD], slot_keys], axis=0)
        values = jnp.concatenate(
            [kv_ref[low:high, first + HD : first + 2 * HD], slot_values], axis=0
        )
        query, grad = stacked(query_ref, tile, head), stacked(grad_ref, tile, head)
        scores = dot_nt(keys, query) + mask
        expo = jnp.exp2((scores - top_ref[at : at + 1, :]) * (SCALE * LOG2E))
        probs = expo * scale_ref[at : at + 1, :]
        dprobs = dot_nt(values, grad)
        dscores = (probs * (dprobs - inner_ref[at : at + 1, :])).astype(BF16)
        weights = probs.astype(BF16)
        attended = dot_tn(values, weights)
        query_grad = dot_tn(keys, dscores) * SCALE
        rows = slice(tile * TILE, (tile + 1) * TILE)
        for j in range(QPK):
            lanes = slice(j * TILE, (j + 1) * TILE)
            columns = slice(j * HD, (j + 1) * HD)
            attended_all[rows, columns] = attended[:, lanes].T.astype(BF16)
            query_grad_all[rows, columns] = query_grad[:, lanes].T.astype(BF16)
        send(0, attended_all, rows, head * QPK * HD)
        send(1, query_grad_all, rows, head * QPK * HD)
        key_part = dot_nn(dscores[: high - low], query)
        value_part = dot_nn(weights[: high - low], grad)
        if tile > 0:
            before = slice((tile - 1) * TILE, tile * TILE)
            kv_grad_all[before, :HD] = ((key_held + key_part[:TILE]) * SCALE).astype(BF16)
            kv_grad_all[before, HD:] = (value_held + value_part[:TILE]).astype(BF16)
            send(2, kv_grad_all, before, first)
        key_held, value_held = key_part[high - low - TILE :], value_part[high - low - TILE :]
    last = slice((tiles - 1) * TILE, tiles * TILE)
    kv_grad_all[last, :HD] = (key_held * SCALE).astype(BF16)
    kv_grad_all[last, HD:] = value_held.astype(BF16)
    send(2, kv_grad_all, last, first)
    for copy in copies:
        copy.wait()


def text_grad(queries, out_grad, text_kv, segment, stats, visual, head, before):
    vmem, hbm = pl.BlockSpec(memory_space=pltpu.VMEM), pl.BlockSpec(memory_space=pltpu.HBM)
    length = queries.shape[0]
    slots = sum(one.shape[0] for one in visual)
    pairs = (slots + 2 * TILE) * length * QPK
    first = 7 + len(visual)
    return pl.pallas_call(
        functools.partial(
            text_grad_kernel, arrivals=len(visual), head=head, held=len(before)
        ),
        out_shape=[
            jax.ShapeDtypeStruct(queries.shape, BF16),
            jax.ShapeDtypeStruct(queries.shape, BF16),
            jax.ShapeDtypeStruct(text_kv.shape, BF16),
        ],
        in_specs=[vmem] * first + [hbm] * len(before),
        out_specs=[hbm] * 3,
        scratch_shapes=[
            pltpu.VMEM((length, QPK * HD), BF16),
            pltpu.VMEM((length, QPK * HD), BF16),
            pltpu.VMEM((length, 2 * HD), BF16),
            pltpu.SemaphoreType.DMA((3 * length // TILE,)),
        ],
        input_output_aliases={first + i: i for i in range(len(before))},
        compiler_params=params(24),
        cost_estimate=cost(12 * pairs * HD, 8 * queries.size, pairs),
        name="text_grad",
    )(queries, out_grad, text_kv, segment, *stats, *visual, *before)


def by_core(weights, body):
    if len(weights) == 1:
        body(weights[0])
    else:
        odd = lax.axis_index("group") & 1
        for parity, weight in enumerate(weights):
            pl.when(odd == parity)(functools.partial(body, weight))


def near_kernel(own_ref, own_weight, part_ref, *refs):
    *weights, out_ref = refs

    def body(weight):
        out_ref[...] = dot_nt(own_ref[...], own_weight[...]) + dot_nt(part_ref[...], weight[...])

    by_core(weights, body)


def far_kernel(before_ref, part_ref, *refs):
    *weights, out_ref = refs

    def body(weight):
        out_ref[...] = before_ref[...] + dot_nt(part_ref[...], weight[...])

    by_core(weights, body)


def feature_grad(kernel, operands, name):
    rows, width = operands[0].shape[0], operands[-1].shape[1]
    features = operands[-1].shape[0]
    vmem = pl.BlockSpec(memory_space=pltpu.VMEM)
    return pl.pallas_call(
        kernel,
        out_shape=jax.ShapeDtypeStruct((rows, features), F32),
        in_specs=[vmem] * len(operands),
        out_specs=vmem,
        compiler_params=params(16),
        cost_estimate=cost(4 * rows * width * features, 4 * width * features),
        name=name,
    )(*operands)


def last_kernel(before_ref, part_ref, *refs):
    *weights, out_ref, rounded, sems = refs
    steps = sems.shape[0]
    count = out_ref.shape[1] // steps

    def copy(step):
        columns = slice(step * count, (step + 1) * count)
        return pltpu.make_async_copy(
            rounded.at[:, columns], out_ref.at[:, columns], sems.at[step]
        )

    def body(weight):
        for step in range(steps):
            columns = slice(step * count, (step + 1) * count)
            term = dot_nt(part_ref[...], weight[columns, :])
            rounded[:, columns] = (before_ref[:, columns] + term).astype(BF16)
            copy(step).start()

    by_core(weights, body)
    for step in range(steps):
        copy(step).wait()


def last_grad(before, part, weights):
    rows, width = part.shape
    features = weights[0].shape[0]
    vmem, hbm = pl.BlockSpec(memory_space=pltpu.VMEM), pl.BlockSpec(memory_space=pltpu.HBM)
    return pl.pallas_call(
        last_kernel,
        out_shape=jax.ShapeDtypeStruct((rows, features), BF16),
        in_specs=[vmem] * (2 + len(weights)),
        out_specs=hbm,
        scratch_shapes=[pltpu.VMEM((rows, features), BF16), pltpu.SemaphoreType.DMA((4,))],
        compiler_params=params(16),
        cost_estimate=cost(2 * rows * width * features, 2 * width * features),
        name="last_grad",
    )(before, part, *weights)


def in_turn(*arrays):
    held = ()
    for array in arrays:
        held = lax.optimization_barrier((*held, array))
    return held


def on_device(
    queries, text_kv, out_grad, text_segment, visual_rows, kv_weight, visual_dest, visual_sample
):
    groups, shares = lax.axis_size("group"), lax.axis_size("tensor")
    rows = visual_rows.shape[0]
    capacity = 2 * rows // groups
    width = kv_weight.shape[1] // shares
    dest_row = visual_dest.reshape(1, rows)
    sample_row = visual_sample.reshape(1, rows)

    columns, after = {}, ()

    def blocks_of(flips, kinds):
        blocks, weights = project(visual_rows, kv_weight, after, width, flips, kinds)
        columns.update(zip(flips, weights, strict=True))
        return blocks

    def across_tensor(block, even_flip, odd_flip):
        pairs = [
            (g * shares + t, g * shares + (t ^ (odd_flip if g % 2 else even_flip)))
            for g in range(groups)
            for t in range(shares)
        ]
        return lax.ppermute(block, ("group", "tensor"), pairs)

    odd = lax.axis_index("group") % 2 == 1
    if shares == 4:
        (far,) = blocks_of([3], [BF16])
        far_landed = across_tensor(far, 1, 1)
        near, cross = blocks_of([1, 2], [BF16, F32])
        after = (cross,)
        (own,) = blocks_of([0], [F32])
        pair = (cross + far_landed.astype(F32)).astype(BF16)
        landed = [
            across_tensor(jnp.where(odd, pair, near), 1, 2),
            across_tensor(jnp.where(odd, near, pair), 2, 1),
        ]
    else:
        flips = list(range(shares - 1, 0, -1))
        landed = [
            across_tensor(block, flip, flip)
            for block, flip in zip(blocks_of(flips, [BF16] * len(flips)), flips, strict=True)
        ]
        (own,) = blocks_of([0], [F32])
    stats = text_stats(queries, out_grad, text_kv, text_segment)
    stats, *landed = in_turn(stats, *landed)

    pairwise = groups == 8
    inputs = (queries, out_grad, text_segment)
    if pairwise:
        ways = [
            [(g, g ^ (odd_flip if g % 2 else even_flip)) for g in range(groups)]
            for even_flip, odd_flip in FLIPS
        ]
        neighbour = [(g, g ^ 1) for g in range(groups)]
        pairs = place(
            dest_row, sample_row, own, landed, capacity, groups * capacity, FLIPS
        )
        pairs = in_turn(
            *[lax.ppermute(pair, "group", way) for pair, way in zip(pairs[:-1], ways[:-1])]
        ) + tuple(pairs[-1:])
        ours = jnp.concatenate([pair[:capacity] for pair in pairs], axis=0)
        theirs = jnp.concatenate([pair[capacity:] for pair in pairs], axis=0)
        theirs = lax.ppermute(theirs, "group", neighbour)
        stats = slot_call(
            slot_stats_kernel, *inputs, ours, stats, False, True, "slot_stats"
        )
        passed, *final = slot_call(
            slot_grad_kernel, *inputs, theirs, stats, True, True, "slot_grad"
        )
        passed = lax.ppermute(passed, "group", neighbour)
        (kept,) = slot_call(
            slot_grad_kernel, *inputs, ours, final, True, False, "slot_grad_kept"
        )
        visual = [ours, theirs]
        passed, final = lax.optimization_barrier((passed, final))
    else:
        (sent,) = place(
            dest_row, sample_row, own, landed, capacity, groups * capacity, None
        )
        visual = [
            lax.all_to_all(
                sent.reshape(groups, capacity, -1), "group", split_axis=0, concat_axis=0, tiled=True
            ).reshape(groups * capacity, -1)
        ]
        kept, *final = slot_call(
            slot_grad_kernel, *inputs, visual[0], stats, True, True, "slot_grad"
        )

    inputs = (queries, out_grad, text_kv, text_segment, final, visual)
    text_outs = text_grad(*inputs, 0, ())

    if pairwise:
        pairs = [
            jnp.concatenate(
                [kept[at * capacity : (at + 1) * capacity], passed[at * capacity : (at + 1) * capacity]],
                axis=0,
            )
            for at in range(len(FLIPS))
        ]
        back = [lax.ppermute(pairs[at], "group", ways[at]) for at in BACK]
        kept, *back = in_turn(text_outs[2], *back)
        text_outs = (*text_outs[:2], kept)
        landed_flips = tuple(FLIPS[at] for at in BACK) + FLIPS[-1:]
        kv_grad = collect(dest_row, back + pairs[-1:], capacity, landed_flips)
    else:
        returned = lax.all_to_all(
            kept.reshape(groups, capacity, -1), "group", split_axis=0, concat_axis=0, tiled=True
        ).reshape(groups * capacity, -1)
        kv_grad = collect(dest_row, [returned], capacity, None)

    for head in range(1, text_kv.shape[1] // (2 * HD)):
        text_outs = text_grad(*inputs, head, text_outs)
    attended, query_grad, text_kv_grad = text_outs

    if shares == 4:
        first = across_tensor(kv_grad, 2, 1)
        second = across_tensor(kv_grad, 1, 2)
        text_kv_grad, second, first = in_turn(text_kv_grad, second, first)
        crossed, near = jnp.where(odd, second, first), jnp.where(odd, first, second)
        gathered = [near, crossed, across_tensor(crossed, 1, 1)]
    else:
        gathered = [across_tensor(kv_grad, flip, flip) for flip in range(1, shares)]
    total = feature_grad(
        near_kernel, (kv_grad, columns[0], gathered[0], columns[1]), "near_grad"
    )
    for flip in range(2, shares - 1):
        total = feature_grad(far_kernel, (total, gathered[flip - 1], columns[flip]), "far_grad")
    total = last_grad(total, gathered[-1], [columns[shares - 1]])
    return (attended, query_grad, text_kv_grad, total)


def solution(mesh):
    placed = (
        P("group", "tensor"),
        P("group", "tensor"),
        P("group", "tensor"),
        P("group", None),
        P("group", "tensor"),
        P("tensor", None),
        P("group", None),
        P("group"),
    )
    return jax.shard_map(
        on_device,
        mesh=mesh,
        in_specs=placed,
        out_specs=(
            P("group", "tensor"),
            P("group", "tensor"),
            P("group", "tensor"),
            P("group", "tensor"),
        ),
        check_vma=False,
    )
```

```python
import functools
import math

import jax
import jax.numpy as jnp
from jax import lax
from jax.experimental import pallas as pl
from jax.experimental.pallas import tpu as pltpu
from jax.sharding import PartitionSpec as P

HD = 128
QPK = 4
TILE = 128
SCALE = 1.0 / math.sqrt(HD)
LOG2E = math.log2(math.e)
F32 = jnp.float32
BF16 = jnp.bfloat16
MIB = 1024 * 1024


def dot_nn(a, b):
    return lax.dot_general(a, b, (((1,), (0,)), ((), ())), preferred_element_type=F32)


def dot_nt(a, b):
    return lax.dot_general(a, b, (((1,), (1,)), ((), ())), preferred_element_type=F32)


def dot_tn(a, b):
    return lax.dot_general(a, b, (((0,), (0,)), ((), ())), preferred_element_type=F32)


def in_hbm(x):
    return pltpu.with_memory_space_constraint(x, pltpu.HBM)


def params(mib):
    return pltpu.CompilerParams(vmem_limit_bytes=mib * MIB)


def cost(flops, moved, exps=0):
    return pl.CostEstimate(flops=flops, bytes_accessed=moved, transcendentals=exps)


def project_kernel(rows_ref, weight_ref, *refs, flips, steps, held):
    count, refs = len(flips), refs[held:]
    outs, weights = refs[:count], refs[count : 2 * count]
    rows, rows_sem, weight_sems = refs[2 * count :]
    here = lax.axis_index("tensor")
    features, width = weights[0].shape
    depth = features // steps
    rows_copy = pltpu.make_async_copy(rows_ref, rows, rows_sem)
    rows_copy.start()
    copies = []
    for at, flip in enumerate(flips):
        first = pl.multiple_of((here ^ flip) * width, width)
        for step in range(steps):
            part = pl.ds(step * depth, depth)
            copy = pltpu.make_async_copy(
                weight_ref.at[part, pl.ds(first, width)],
                weights[at].at[part],
                weight_sems.at[at, step],
            )
            copy.start()
            copies.append(copy)
    rows_copy.wait()
    for at, out in enumerate(outs):
        total = None
        for step in range(steps):
            copies[at * steps + step].wait()
            part = slice(step * depth, (step + 1) * depth)
            term = dot_nn(rows[:, part], weights[at][part, :])
            total = term if total is None else total + term
        out[...] = total.astype(out.dtype)


def project(rows, weight, after, width, flips, kinds):
    count, features = rows.shape
    steps = 4
    vmem, hbm = pl.BlockSpec(memory_space=pltpu.VMEM), pl.BlockSpec(memory_space=pltpu.HBM)
    found = pl.pallas_call(
        functools.partial(project_kernel, flips=flips, steps=steps, held=len(after)),
        out_shape=[jax.ShapeDtypeStruct((count, width), kind) for kind in kinds]
        + [jax.ShapeDtypeStruct((features, width), BF16) for _ in kinds],
        in_specs=[hbm, hbm] + [pl.BlockSpec(memory_space=pl.ANY)] * len(after),
        out_specs=[vmem] * (2 * len(kinds)),
        scratch_shapes=[
            pltpu.VMEM((count, features), BF16),
            pltpu.SemaphoreType.DMA,
            pltpu.SemaphoreType.DMA((len(kinds), steps)),
        ],
        compiler_params=params(16),
        cost_estimate=cost(
            2 * count * features * width * len(kinds), 2 * features * width * len(kinds)
        ),
        name="project",
    )(in_hbm(rows), in_hbm(weight), *after)
    return found[: len(kinds)], found[len(kinds) :]


FLIPS = ((6, 6), (4, 2), (2, 4), (0, 0))
BACK = (0, 2, 1)


def target_of(slot, capacity, flips):
    if flips is None:
        return slot // capacity
    me = lax.axis_index("group")
    odd = me & 1
    chip = jnp.zeros(slot.shape, jnp.int32)
    for at, (even_flip, odd_flip) in enumerate(flips):
        pack = me ^ jnp.where(odd == 1, odd_flip, even_flip)
        chip = jnp.where(slot // (2 * capacity) == at, pack, chip)
    return chip ^ ((slot // capacity) & 1)


def place_kernel(dest_ref, sample_ref, own_ref, *refs, capacity, flips, count):
    parts, outs = refs[:-count], refs[-count:]
    total = own_ref[...]
    for part in parts:
        total = total + part[...].astype(F32)
    rows = total.shape[0]
    tags = jnp.broadcast_to(sample_ref[...] + 1, (TILE, rows)).astype(F32).T
    wide = jnp.concatenate([total, tags], axis=1).astype(BF16)
    each = outs[0].shape[0]
    slot = lax.broadcasted_iota(jnp.int32, (each * count, rows), 0)
    row = lax.broadcasted_iota(jnp.int32, (each * count, rows), 1)
    target = target_of(slot, capacity, flips)
    select = (dest_ref[...] == target) & (slot % capacity == row % capacity)
    placed = dot_nn(select.astype(F32).astype(BF16), wide).astype(BF16)
    for at, out in enumerate(outs):
        out[...] = placed[at * each : (at + 1) * each]


def place(dest_row, sample_row, own, parts, capacity, slots, flips):
    rows, width = own.shape
    count = len(flips) if flips else 1
    vmem = pl.BlockSpec(memory_space=pltpu.VMEM)
    return pl.pallas_call(
        functools.partial(place_kernel, capacity=capacity, flips=flips, count=count),
        out_shape=[jax.ShapeDtypeStruct((slots // count, width + TILE), BF16)] * count,
        in_specs=[vmem] * (3 + len(parts)),
        out_specs=[vmem] * count,
        compiler_params=params(8),
        cost_estimate=cost(2 * slots * rows * width, 4 * rows * width),
        name="place",
    )(dest_row, sample_row, own, *parts)


def collect_kernel(dest_ref, *refs, capacity, flips):
    parts, out = refs[:-1], refs[-1]
    rows = out.shape[0]
    grads = jnp.concatenate([part[...] for part in parts], axis=0)
    slots = grads.shape[0]
    slot = lax.broadcasted_iota(jnp.int32, (rows, slots), 1)
    row = lax.broadcasted_iota(jnp.int32, (rows, slots), 0)
    target = target_of(slot, capacity, flips)
    dest = jnp.broadcast_to(dest_ref[...], (slots, rows)).astype(F32).T
    select = (dest == target.astype(F32)) & (slot % capacity == row % capacity)
    out[...] = dot_nn(select.astype(F32).astype(BF16), grads).astype(BF16)


def collect(dest_row, parts, capacity, flips):
    rows, width = dest_row.shape[1], parts[0].shape[1]
    vmem = pl.BlockSpec(memory_space=pltpu.VMEM)
    return pl.pallas_call(
        functools.partial(collect_kernel, capacity=capacity, flips=flips),
        out_shape=jax.ShapeDtypeStruct((rows, width), BF16),
        in_specs=[vmem] * (1 + len(parts)),
        out_specs=vmem,
        compiler_params=params(8),
        cost_estimate=cost(2 * 256 * rows * width, 4 * rows * width),
        name="collect",
    )(dest_row, *parts)


def stacked(ref, tile, head):
    first = head * QPK * HD
    return jnp.concatenate(
        [
            ref[tile * TILE : (tile + 1) * TILE, first + j * HD : first + (j + 1) * HD]
            for j in range(QPK)
        ],
        axis=0,
    )


def text_span(tile):
    return max(0, tile - 1) * TILE, (tile + 1) * TILE


def text_mask(segment_ref, tile):
    low, high = text_span(tile)
    span = high - low
    own = segment_ref[:, tile * TILE : (tile + 1) * TILE].astype(F32)
    keys = jnp.concatenate(
        [
            jnp.broadcast_to(segment_ref[:, at : at + TILE].astype(F32), (TILE, TILE)).T
            for at in range(low, high, TILE)
        ],
        axis=0,
    )
    key_place = lax.broadcasted_iota(jnp.int32, (span, TILE), 0) + low
    token_place = lax.broadcasted_iota(jnp.int32, (span, TILE), 1) + tile * TILE
    mask = (keys == own) & (key_place <= token_place)
    return jnp.where(mask, 0.0, -jnp.inf)


def slot_mask(tags, segment_ref, tile):
    own = segment_ref[:, tile * TILE : (tile + 1) * TILE].astype(F32) + 1.0
    return jnp.where(tags.astype(F32) == own, 0.0, -jnp.inf)


def repeated(mask):
    return jnp.concatenate([mask] * QPK, axis=1)


def text_stats_kernel(query_ref, grad_ref, kv_ref, segment_ref, top_ref, sum_ref, inner_ref):
    tiles, heads = query_ref.shape[0] // TILE, kv_ref.shape[1] // (2 * HD)
    for tile in range(tiles):
        low, high = text_span(tile)
        mask = repeated(text_mask(segment_ref, tile))
        for head in range(heads):
            at = head * tiles + tile
            keys = kv_ref[low:high, head * 2 * HD : head * 2 * HD + HD]
            values = kv_ref[low:high, head * 2 * HD + HD : (head + 1) * 2 * HD]
            scores = dot_nt(keys, stacked(query_ref, tile, head)) + mask
            top = jnp.max(scores, axis=0, keepdims=True)
            expo = jnp.exp2((scores - top) * (SCALE * LOG2E))
            dprobs = dot_nt(values, stacked(grad_ref, tile, head))
            top_ref[at : at + 1, :] = top
            sum_ref[at : at + 1, :] = jnp.sum(expo, axis=0, keepdims=True)
            inner_ref[at : at + 1, :] = jnp.sum(expo * dprobs, axis=0, keepdims=True)


def text_stats(queries, out_grad, text_kv, segment):
    tiles, heads = queries.shape[0] // TILE, text_kv.shape[1] // (2 * HD)
    vmem = pl.BlockSpec(memory_space=pltpu.VMEM)
    shape = jax.ShapeDtypeStruct((tiles * heads, QPK * TILE), F32)
    pairs = heads * QPK * (2 * tiles - 1) * TILE * TILE
    return pl.pallas_call(
        text_stats_kernel,
        out_shape=[shape] * 3,
        in_specs=[vmem] * 4,
        out_specs=[vmem] * 3,
        compiler_params=params(24),
        cost_estimate=cost(4 * pairs * HD, 4 * queries.size, pairs),
        name="text_stats",
    )(queries, out_grad, text_kv, segment)


def slot_tiles(query_ref, grad_ref, segment_ref, slots_ref):
    tiles = query_ref.shape[0] // TILE
    width = slots_ref.shape[1] - TILE
    masks = [
        repeated(slot_mask(slots_ref[:, width:], segment_ref, tile)) for tile in range(tiles)
    ]
    for head in range(width // (2 * HD)):
        first = head * 2 * HD
        keys = slots_ref[:, first : first + HD]
        values = slots_ref[:, first + HD : first + 2 * HD]
        for tile in range(tiles):
            query, grad = stacked(query_ref, tile, head), stacked(grad_ref, tile, head)
            scores = dot_nt(keys, query) + masks[tile]
            yield head, tile, head * tiles + tile, query, grad, scores, dot_nt(values, grad)


def joined(scores, dprobs, top_ref, sum_ref, inner_ref, at):
    before = top_ref[at : at + 1, :]
    top = jnp.maximum(before, jnp.max(scores, axis=0, keepdims=True))
    expo = jnp.exp2((scores - top) * (SCALE * LOG2E))
    shift = jnp.exp2((before - top) * (SCALE * LOG2E))
    total = sum_ref[at : at + 1, :] * shift + jnp.sum(expo, axis=0, keepdims=True)
    inner = inner_ref[at : at + 1, :] * shift + jnp.sum(expo * dprobs, axis=0, keepdims=True)
    return expo, top, total, inner


def slot_stats_kernel(
    query_ref, grad_ref, segment_ref, slots_ref, top_ref, sum_ref, inner_ref, *outs
):
    for _, _, at, _, _, scores, dprobs in slot_tiles(query_ref, grad_ref, segment_ref, slots_ref):
        found = joined(scores, dprobs, top_ref, sum_ref, inner_ref, at)
        for out, row in zip(outs, found[1:], strict=True):
            out[at : at + 1, :] = row


def slot_grad_kernel(
    query_ref, grad_ref, segment_ref, slots_ref, top_ref, sum_ref, inner_ref, out_ref, *outs
):
    tiles, slots = query_ref.shape[0] // TILE, slots_ref.shape[0]
    for head, tile, at, query, grad, scores, dprobs in slot_tiles(
        query_ref, grad_ref, segment_ref, slots_ref
    ):
        if outs:
            expo, top, total, inner = joined(scores, dprobs, top_ref, sum_ref, inner_ref, at)
            inverse = 1.0 / total
            inner = inner * inverse
            for out, row in zip(outs, (top, inverse, inner), strict=True):
                out[at : at + 1, :] = row
        else:
            expo = jnp.exp2((scores - top_ref[at : at + 1, :]) * (SCALE * LOG2E))
            inverse, inner = sum_ref[at : at + 1, :], inner_ref[at : at + 1, :]
        probs = expo * inverse
        dscores = (probs * (dprobs - inner)).astype(BF16)
        value_part = dot_nn(probs.astype(BF16), grad)
        key_part = dot_nn(dscores, query)
        value_grad = value_part if tile == 0 else value_grad + value_part
        key_grad = key_part if tile == 0 else key_grad + key_part
        if tile == tiles - 1:
            first = head * 2 * HD
            out_ref[:, first : first + HD] = (key_grad * SCALE).astype(BF16)
            out_ref[:, first + HD : first + 2 * HD] = value_grad.astype(BF16)


def slot_call(kernel, queries, out_grad, segment, slots, stats, grads, joins, name):
    vmem = pl.BlockSpec(memory_space=pltpu.VMEM)
    pairs = slots.shape[0] * queries.shape[0] * queries.shape[1] // HD
    shapes = []
    if grads:
        shapes.append(jax.ShapeDtypeStruct((slots.shape[0], slots.shape[1] - TILE), BF16))
    if joins:
        shapes += [jax.ShapeDtypeStruct(stats[0].shape, F32)] * 3
    return pl.pallas_call(
        kernel,
        out_shape=shapes,
        in_specs=[vmem] * 7,
        out_specs=[vmem] * len(shapes),
        compiler_params=params(24),
        cost_estimate=cost((8 if grads else 4) * pairs * HD, 4 * queries.size, pairs),
        name=name,
    )(queries, out_grad, segment, slots, *stats)


def text_grad_kernel(
    query_ref,
    grad_ref,
    kv_ref,
    segment_ref,
    top_ref,
    scale_ref,
    inner_ref,
    *refs,
    arrivals,
    head,
    held,
):
    visual, refs = refs[:arrivals], refs[arrivals + held :]
    outs, (attended_all, query_grad_all, kv_grad_all, sems) = refs[:3], refs[3:]
    tiles, width = query_ref.shape[0] // TILE, kv_ref.shape[1]
    first = head * 2 * HD
    tags = jnp.concatenate([one[:, width:] for one in visual], axis=0)
    slot_keys = jnp.concatenate([one[:, first : first + HD] for one in visual], axis=0)
    slot_values = jnp.concatenate([one[:, first + HD : first + 2 * HD] for one in visual], axis=0)
    key_held = value_held = None
    copies = []

    def send(which, held, rows, start):
        copy = pltpu.make_async_copy(
            held.at[rows],
            outs[which].at[rows, start : start + held.shape[1]],
            sems.at[len(copies)],
        )
        copy.start()
        copies.append(copy)

    for tile in range(tiles):
        at = head * tiles + tile
        low, high = text_span(tile)
        mask = repeated(
            jnp.concatenate(
                [text_mask(segment_ref, tile), slot_mask(tags, segment_ref, tile)], axis=0
            )
        )
        keys = jnp.concatenate([kv_ref[low:high, first : first + HD], slot_keys], axis=0)
        values = jnp.concatenate(
            [kv_ref[low:high, first + HD : first + 2 * HD], slot_values], axis=0
        )
        query, grad = stacked(query_ref, tile, head), stacked(grad_ref, tile, head)
        scores = dot_nt(keys, query) + mask
        expo = jnp.exp2((scores - top_ref[at : at + 1, :]) * (SCALE * LOG2E))
        probs = expo * scale_ref[at : at + 1, :]
        dprobs = dot_nt(values, grad)
        dscores = (probs * (dprobs - inner_ref[at : at + 1, :])).astype(BF16)
        weights = probs.astype(BF16)
        attended = dot_tn(values, weights)
        query_grad = dot_tn(keys, dscores) * SCALE
        rows = slice(tile * TILE, (tile + 1) * TILE)
        for j in range(QPK):
            lanes = slice(j * TILE, (j + 1) * TILE)
            columns = slice(j * HD, (j + 1) * HD)
            attended_all[rows, columns] = attended[:, lanes].T.astype(BF16)
            query_grad_all[rows, columns] = query_grad[:, lanes].T.astype(BF16)
        send(0, attended_all, rows, head * QPK * HD)
        send(1, query_grad_all, rows, head * QPK * HD)
        key_part = dot_nn(dscores[: high - low], query)
        value_part = dot_nn(weights[: high - low], grad)
        if tile > 0:
            before = slice((tile - 1) * TILE, tile * TILE)
            kv_grad_all[before, :HD] = ((key_held + key_part[:TILE]) * SCALE).astype(BF16)
            kv_grad_all[before, HD:] = (value_held + value_part[:TILE]).astype(BF16)
            send(2, kv_grad_all, before, first)
        key_held, value_held = key_part[high - low - TILE :], value_part[high - low - TILE :]
    last = slice((tiles - 1) * TILE, tiles * TILE)
    kv_grad_all[last, :HD] = (key_held * SCALE).astype(BF16)
    kv_grad_all[last, HD:] = value_held.astype(BF16)
    send(2, kv_grad_all, last, first)
    for copy in copies:
        copy.wait()


def text_grad(queries, out_grad, text_kv, segment, stats, visual, head, before):
    vmem, hbm = pl.BlockSpec(memory_space=pltpu.VMEM), pl.BlockSpec(memory_space=pltpu.HBM)
    length = queries.shape[0]
    slots = sum(one.shape[0] for one in visual)
    pairs = (slots + 2 * TILE) * length * QPK
    first = 7 + len(visual)
    return pl.pallas_call(
        functools.partial(
            text_grad_kernel, arrivals=len(visual), head=head, held=len(before)
        ),
        out_shape=[
            jax.ShapeDtypeStruct(queries.shape, BF16),
            jax.ShapeDtypeStruct(queries.shape, BF16),
            jax.ShapeDtypeStruct(text_kv.shape, BF16),
        ],
        in_specs=[vmem] * first + [hbm] * len(before),
        out_specs=[hbm] * 3,
        scratch_shapes=[
            pltpu.VMEM((length, QPK * HD), BF16),
            pltpu.VMEM((length, QPK * HD), BF16),
            pltpu.VMEM((length, 2 * HD), BF16),
            pltpu.SemaphoreType.DMA((3 * length // TILE,)),
        ],
        input_output_aliases={first + i: i for i in range(len(before))},
        compiler_params=params(24),
        cost_estimate=cost(12 * pairs * HD, 8 * queries.size, pairs),
        name="text_grad",
    )(queries, out_grad, text_kv, segment, *stats, *visual, *before)


def crossed_kernel(first_ref, second_ref, out_ref):
    odd = lax.axis_index("group") & 1 == 1
    out_ref[...] = jnp.where(odd, second_ref[...], first_ref[...])


def crossed_of(first, second):
    vmem = pl.BlockSpec(memory_space=pltpu.VMEM)
    return pl.pallas_call(
        crossed_kernel,
        out_shape=jax.ShapeDtypeStruct(first.shape, BF16),
        in_specs=[vmem] * 2,
        out_specs=vmem,
        compiler_params=params(8),
        cost_estimate=cost(first.size, 6 * first.size),
        name="crossed",
    )(first, second)


def near_kernel(own_ref, own_weight, first_ref, second_ref, weight_ref, out_ref):
    odd = lax.axis_index("group") & 1 == 1
    near = jnp.where(odd, first_ref[...], second_ref[...])
    out_ref[...] = dot_nt(own_ref[...], own_weight[...]) + dot_nt(near, weight_ref[...])


def next_kernel(before_ref, part_ref, weight_ref, out_ref):
    out_ref[...] = before_ref[...] + dot_nt(part_ref[...], weight_ref[...])


def feature_grad(kernel, operands, name):
    rows, width = operands[0].shape[0], operands[-1].shape[1]
    features = operands[-1].shape[0]
    vmem = pl.BlockSpec(memory_space=pltpu.VMEM)
    return pl.pallas_call(
        kernel,
        out_shape=jax.ShapeDtypeStruct((rows, features), F32),
        in_specs=[vmem] * len(operands),
        out_specs=vmem,
        compiler_params=params(16),
        cost_estimate=cost(4 * rows * width * features, 4 * width * features),
        name=name,
    )(*operands)


def turn_kernel(weight_ref, out_ref):
    for start in range(0, weight_ref.shape[0], 2 * TILE):
        out_ref[:, start : start + 2 * TILE] = weight_ref[start : start + 2 * TILE, :].T


def turn(weight):
    features, width = weight.shape
    vmem = pl.BlockSpec(memory_space=pltpu.VMEM)
    return pl.pallas_call(
        turn_kernel,
        out_shape=jax.ShapeDtypeStruct((width, features), BF16),
        in_specs=[vmem],
        out_specs=vmem,
        compiler_params=params(16),
        cost_estimate=cost(0, 4 * width * features),
        name="turn",
    )(weight)


def last_kernel(before_ref, part_ref, weight_ref, out_ref, rounded, sems):
    steps = sems.shape[0]
    count = out_ref.shape[1] // steps
    copies = []
    for step in range(steps):
        columns = slice(step * count, (step + 1) * count)
        term = dot_nn(part_ref[...], weight_ref[:, columns])
        rounded[:, columns] = (before_ref[:, columns] + term).astype(BF16)
        copies.append(
            pltpu.make_async_copy(
                rounded.at[:, columns], out_ref.at[:, columns], sems.at[step]
            )
        )
        copies[-1].start()
    for copy in copies:
        copy.wait()


def last_grad(before, part, weight):
    rows, width = part.shape
    features = weight.shape[1]
    vmem, hbm = pl.BlockSpec(memory_space=pltpu.VMEM), pl.BlockSpec(memory_space=pltpu.HBM)
    return pl.pallas_call(
        last_kernel,
        out_shape=jax.ShapeDtypeStruct((rows, features), BF16),
        in_specs=[vmem] * 3,
        out_specs=hbm,
        scratch_shapes=[pltpu.VMEM((rows, features), BF16), pltpu.SemaphoreType.DMA((4,))],
        compiler_params=params(16),
        cost_estimate=cost(2 * rows * width * features, 2 * width * features),
        name="last_grad",
    )(before, part, weight)


def in_turn(*arrays):
    held = ()
    for array in arrays:
        held = lax.optimization_barrier((*held, array))
    return held


def on_device(
    queries, text_kv, out_grad, text_segment, visual_rows, kv_weight, visual_dest, visual_sample
):
    groups, shares = lax.axis_size("group"), lax.axis_size("tensor")
    rows = visual_rows.shape[0]
    capacity = 2 * rows // groups
    width = kv_weight.shape[1] // shares
    dest_row = visual_dest.reshape(1, rows)
    sample_row = visual_sample.reshape(1, rows)

    columns, after = {}, ()

    def blocks_of(flips, kinds):
        blocks, weights = project(visual_rows, kv_weight, after, width, flips, kinds)
        columns.update(zip(flips, weights, strict=True))
        return blocks

    def across_tensor(block, even_flip, odd_flip):
        pairs = [
            (g * shares + t, g * shares + (t ^ (odd_flip if g % 2 else even_flip)))
            for g in range(groups)
            for t in range(shares)
        ]
        return lax.ppermute(block, ("group", "tensor"), pairs)

    odd = lax.axis_index("group") % 2 == 1
    if shares == 4:
        (far,) = blocks_of([3], [BF16])
        far_landed = across_tensor(far, 1, 1)
        near, cross = blocks_of([1, 2], [BF16, F32])
        after = (cross,)
        (own,) = blocks_of([0], [F32])
        pair = (cross + far_landed.astype(F32)).astype(BF16)
        landed = [
            across_tensor(jnp.where(odd, pair, near), 1, 2),
            across_tensor(jnp.where(odd, near, pair), 2, 1),
        ]
    else:
        flips = list(range(shares - 1, 0, -1))
        landed = [
            across_tensor(block, flip, flip)
            for block, flip in zip(blocks_of(flips, [BF16] * len(flips)), flips, strict=True)
        ]
        (own,) = blocks_of([0], [F32])
    stats = text_stats(queries, out_grad, text_kv, text_segment)
    stats, *landed = in_turn(stats, *landed)

    pairwise = groups == 8
    inputs = (queries, out_grad, text_segment)
    if pairwise:
        ways = [
            [(g, g ^ (odd_flip if g % 2 else even_flip)) for g in range(groups)]
            for even_flip, odd_flip in FLIPS
        ]
        neighbour = [(g, g ^ 1) for g in range(groups)]
        pairs = place(
            dest_row, sample_row, own, landed, capacity, groups * capacity, FLIPS
        )
        pairs = in_turn(
            *[lax.ppermute(pair, "group", way) for pair, way in zip(pairs[:-1], ways[:-1])]
        ) + tuple(pairs[-1:])
        ours = jnp.concatenate([pair[:capacity] for pair in pairs], axis=0)
        theirs = jnp.concatenate([pair[capacity:] for pair in pairs], axis=0)
        theirs = lax.ppermute(theirs, "group", neighbour)
        stats = slot_call(
            slot_stats_kernel, *inputs, ours, stats, False, True, "slot_stats"
        )
        passed, *final = slot_call(
            slot_grad_kernel, *inputs, theirs, stats, True, True, "slot_grad"
        )
        passed = lax.ppermute(passed, "group", neighbour)
        (kept,) = slot_call(
            slot_grad_kernel, *inputs, ours, final, True, False, "slot_grad_kept"
        )
        visual = [ours, theirs]
        passed, final = lax.optimization_barrier((passed, final))
    else:
        (sent,) = place(
            dest_row, sample_row, own, landed, capacity, groups * capacity, None
        )
        visual = [
            lax.all_to_all(
                sent.reshape(groups, capacity, -1), "group", split_axis=0, concat_axis=0, tiled=True
            ).reshape(groups * capacity, -1)
        ]
        kept, *final = slot_call(
            slot_grad_kernel, *inputs, visual[0], stats, True, True, "slot_grad"
        )

    inputs = (queries, out_grad, text_kv, text_segment, final, visual)
    text_outs = text_grad(*inputs, 0, ())

    if pairwise:
        pairs = [
            jnp.concatenate(
                [kept[at * capacity : (at + 1) * capacity], passed[at * capacity : (at + 1) * capacity]],
                axis=0,
            )
            for at in range(len(FLIPS))
        ]
        back = [lax.ppermute(pairs[at], "group", ways[at]) for at in BACK]
        kept, *back = in_turn(text_outs[2], *back)
        text_outs = (*text_outs[:2], kept)
        landed_flips = tuple(FLIPS[at] for at in BACK) + FLIPS[-1:]
        kv_grad = collect(dest_row, back + pairs[-1:], capacity, landed_flips)
    else:
        returned = lax.all_to_all(
            kept.reshape(groups, capacity, -1), "group", split_axis=0, concat_axis=0, tiled=True
        ).reshape(groups * capacity, -1)
        kv_grad = collect(dest_row, [returned], capacity, None)

    for head in range(1, text_kv.shape[1] // (2 * HD)):
        text_outs = text_grad(*inputs, head, text_outs)
    attended, query_grad, text_kv_grad = text_outs

    if shares == 4:
        first = across_tensor(kv_grad, 2, 1)
        second = across_tensor(kv_grad, 1, 2)
        text_kv_grad, turned, second, first = in_turn(
            text_kv_grad, turn(columns[shares - 1]), second, first
        )
        crossed = crossed_of(first, second)
        last = across_tensor(crossed, 1, 1)
        operands = (kv_grad, columns[0], first, second, columns[1])
        total = feature_grad(near_kernel, operands, "near_grad")
        total = feature_grad(next_kernel, (total, crossed, columns[2]), "next_grad")
    else:
        *gathered, last = [across_tensor(kv_grad, flip, flip) for flip in range(1, shares)]
        turned = turn(columns[shares - 1])
        total = jnp.zeros((rows, kv_weight.shape[0]), F32)
        for flip, part in enumerate([kv_grad, *gathered]):
            total = feature_grad(next_kernel, (total, part, columns[flip]), "next_grad")
    total = last_grad(total, last, turned)
    return (attended, query_grad, text_kv_grad, total)


def solution(mesh):
    placed = (
        P("group", "tensor"),
        P("group", "tensor"),
        P("group", "tensor"),
        P("group", None),
        P("group", "tensor"),
        P("tensor", None),
        P("group", None),
        P("group"),
    )
    return jax.shard_map(
        on_device,
        mesh=mesh,
        in_specs=placed,
        out_specs=(
            P("group", "tensor"),
            P("group", "tensor"),
            P("group", "tensor"),
            P("group", "tensor"),
        ),
        check_vma=False,
    )
```
